256 devices in a mesh: span: 64 (over z, x, core), cross: 4 (over y).
Axes of the slice: x: 4, y: 4, z: 8, core: 2. Of those that a mesh axis runs over, the one named last changes fastest.
Arguments:
- populations: bfloat16 [19, 1024, 128, 128], P(None, 'span', 'cross'), may hold values from 0.2 to 1.8
- cell_index: int32 [32768, 8], P(('span', 'cross')), may hold values from 0 to 65535
- marker_weight: float32 [32768, 8], P(('span', 'cross')), may hold values from 0 to 0.25
- segment_id: int32 [32768], P(('span', 'cross')), may hold values from 0 to 2047, as said below
Outputs:
- populations_next: bfloat16 [19, 1024, 128, 128], P(None, 'span', 'cross')
- eddy_coeff: float32 [128, 128], P('cross')
- segment_force: float32 [3, 2048], P(None, ('span', 'cross'))
The draws below stay inside these ranges and needn't reach their ends.
Inputs may be any that keep to these rules, and one draw needn't show every extreme that they name: cell_index addresses a cell of the block of the device that holds the marker, flat in the order (span, crossflow, stream) of that 16 x 32 x 128 block. `segment_id`: segments are owned 8 to a device in device order (span slowest); a marker's segment may be owned by any device.
All inputs are finite; a program needn't handle non-finite values.
Results may differ from the reference program's by a relative error of at most 0.0019.
The reference program's roundings to bfloat16 on the way (of `post`) count: a program that leaves them out, or rounds other values in their place, can miss the bound.
Values may be sent and summed in bfloat16 or wider, within the bound.
A program may use at most 128 MiB of HBM per device.

```python
import jax
import jax.numpy as jnp
from jax import lax

Q = 19
CX = 128
CY = 32
CZ = 16
MK_DEV = 128
SEG_DEV = 8
K = 8
NY = 128
NZ = 1024
MARKERS = 32768
SEGMENTS = 2048
N_SPAN = 64
N_CROSS = 4


def draw_populations(key, part):
    key = jax.random.fold_in(key, 23)
    span_frac = jnp.arange(NZ, dtype=jnp.float32) / max(NZ - 1, 1)
    first = jnp.sin(0.5 * jnp.pi * jax.random.uniform(jax.random.fold_in(key, 1), (Q, 1, NY, CX), jnp.float32, -1.0, 1.0))
    second = jnp.sin(0.5 * jnp.pi * jax.random.uniform(jax.random.fold_in(key, 2), (Q, 1, NY, CX), jnp.float32, -1.0, 1.0))
    tile_low = -1.0
    rough_low = 0.5
    mixing = (0.15 + 0.85 * span_frac) * jax.random.uniform(jax.random.fold_in(key, 3), (NZ,), jnp.float32, rough_low, 1.0)
    mixing = mixing[None, :, None, None]
    noise = jax.random.uniform(jax.random.fold_in(key, 4), (Q, NZ, NY, CX), jnp.float32, -1.0, 1.0)
    shaped = 0.8 * (mixing * first + (1.0 - mixing) * second) + 0.2 * noise
    tiles = jax.random.uniform(jax.random.fold_in(key, 5), (NY // 4 + 1, CX // 4 + 1), jnp.float32, tile_low, 0.0)
    tile_rows = jnp.arange(NY, dtype=jnp.int32) // 4
    tile_cols = jnp.arange(CX, dtype=jnp.int32) // 4
    tile_env = jnp.exp(tiles[tile_rows][:, tile_cols])
    span_env = jnp.exp(0.5 * (span_frac - 1.0))
    pops = 1.0 + 0.8 * span_env[None, :, None, None] * tile_env[None, None] * shaped
    return pops.astype(jnp.bfloat16)


def draw_segment_id(key, part):
    key = jax.random.fold_in(key, 11)
    owners = SEGMENTS // SEG_DEV
    marker = jnp.arange(MARKERS, dtype=jnp.int32)
    device = marker // MK_DEV
    local = marker % MK_DEV
    random_owner = jax.random.randint(jax.random.fold_in(key, 1), (MARKERS,), 0, owners)
    far_owner = (device + owners // 2) % owners
    prior_owner = (device + owners - 1) % owners
    owner = jnp.where(local == 0, far_owner, jnp.where(local == 1, prior_owner, random_owner))
    within = jax.random.randint(jax.random.fold_in(key, 2), (MARKERS,), 0, SEG_DEV)
    segment = owner * SEG_DEV + within
    segment = jnp.where(marker == 2, SEGMENTS - 1, segment)
    segment = jnp.where(marker == 3, 0, segment)
    return segment.astype(jnp.int32)


def with_ends(entries, rng, low, top_value):
    longest = entries.shape.index(max(entries.shape))
    spots = []
    for shift in (0, 1):
        where = [jax.random.randint(jax.random.fold_in(rng, axis), (), 0, length) for axis, length in enumerate(entries.shape)]
        where[longest] = (where[longest] + shift) % entries.shape[longest]
        spots.append(tuple(where))
    return entries.at[spots[0]].set(low).at[spots[1]].set(top_value)


def level_of(stream_key, dims, shards, low, high):
    level = 1.0
    for axis_at, shards_of in shards:
        draws = jax.random.uniform(jax.random.fold_in(jax.random.fold_in(stream_key, 6), axis_at), (shards_of,), jnp.float32, low / len(shards), high / len(shards))
        level = level * jnp.repeat(jnp.exp(draws), dims[axis_at] // shards_of).reshape((-1,) + (1,) * (len(dims) - 1 - axis_at))
    return level


def setup_inputs(seed: int = 0) -> dict:
    arg_keys = jax.random.split(jax.random.key(seed), 5)
    populations = draw_populations(jax.random.fold_in(arg_keys[4], 71), 0)
    cell_index = with_ends(jax.random.randint(arg_keys[1], (MARKERS, K), 0, CZ * CY * CX), jax.random.fold_in(arg_keys[1], 1), 0, (CZ * CY * CX) - 1).astype(jnp.int32)
    marker_weight = jnp.clip(0.25 * jax.random.uniform(arg_keys[2], (MARKERS, K), jnp.float32) ** level_of(arg_keys[2], (MARKERS, K), ((0, 256),), -0.2, 0.2), 0.0, 0.25)
    segment_id = draw_segment_id(jax.random.fold_in(arg_keys[4], 71), 0)
    return dict(populations=populations, cell_index=cell_index, marker_weight=marker_weight, segment_id=segment_id)


eps_sum = 1e-06
base_visc = 0.005

def lattice_tables():
    velocities = [[0, 0, 0], [1, 0, 0], [-1, 0, 0], [0, 1, 0], [0, -1, 0], [0, 0, 1], [0, 0, -1], [1, 1, 0], [-1, -1, 0], [1, -1, 0], [-1, 1, 0], [1, 0, 1], [-1, 0, -1], [1, 0, -1], [-1, 0, 1], [0, 1, 1], [0, -1, -1], [0, 1, -1], [0, -1, 1]]
    weights = [1.0 / 3.0] + [1.0 / 18.0] * 6 + [1.0 / 36.0] * 12
    return (velocities, weights)

def inner_product(first, second):
    return sum((first[index] * second[index] for index in range(19)))

def relax_tables():
    velocities, weights = lattice_tables()
    along_x = [float(entry[0]) for entry in velocities]
    along_y = [float(entry[1]) for entry in velocities]
    along_z = [float(entry[2]) for entry in velocities]
    polynomials = []
    for index in range(19):
        cx, cy, cz = (along_x[index], along_y[index], along_z[index])
        square = cx * cx + cy * cy + cz * cz
        normal_x = 3.0 * cx * cx - square
        normal_yz = cy * cy - cz * cz
        polynomials.append([1.0, square, square * square, cx, cx * square, cy, cy * square, cz, cz * square, normal_x, normal_x * square, normal_yz, normal_yz * square, cx * cy, cy * cz, cx * cz, cx * (cy * cy - cz * cz), cy * (cz * cz - cx * cx), cz * (cx * cx - cy * cy)])
    ortho_rows = []
    for moment in range(19):
        vector = [polynomials[index][moment] for index in range(19)]
        for prior in ortho_rows:
            factor = inner_product(vector, prior) / inner_product(prior, prior)
            vector = [vector[index] - factor * prior[index] for index in range(19)]
        ortho_rows.append(vector)
    norms = [inner_product(row_vec, row_vec) for row_vec in ortho_rows]
    fixed = [0.0, 1.19, 1.4, 0.0, 1.2, 0.0, 1.2, 0.0, 1.2, 0.0, 1.4, 0.0, 1.4, 0.0, 0.0, 0.0, 1.98, 1.98, 1.98]
    shear = [1.0 if moment in (9, 11, 13, 14, 15) else 0.0 for moment in range(19)]

    def build(rates):
        return [[sum((ortho_rows[moment][outer] / norms[moment] * rates[moment] * ortho_rows[moment][inner] for moment in range(19))) for inner in range(19)] for outer in range(19)]
    return (build(fixed), build(shear))

def moment_basis():
    velocities, weights = lattice_tables()
    return [[1.0] * 19] + [[float(entry[dim]) for entry in velocities] for dim in range(3)]

def moments(pops):
    basis = jnp.asarray(moment_basis(), jnp.bfloat16)
    sums = jnp.dot(basis, pops.reshape(19, -1), preferred_element_type=jnp.float32)
    density = sums[0]
    return (density, sums[1:] / density)

def collide(pops, density, velocity, rate):
    velocities, weights = lattice_tables()
    fixed_mat, shear_mat = relax_tables()
    flat = pops.reshape(19, -1).astype(jnp.float32)
    along = jnp.dot(jnp.asarray(velocities, jnp.float32), velocity, precision=lax.Precision.HIGHEST)
    speed = lax.optimization_barrier(jnp.sum(velocity * velocity, axis=0))
    equil = jnp.asarray(weights, jnp.float32)[:, None] * density * (1.0 + 3.0 * along + 4.5 * along * along - 1.5 * speed)
    offeq = flat - equil
    relaxed = jnp.dot(jnp.asarray(fixed_mat, jnp.float32), offeq, precision=lax.Precision.HIGHEST)
    sheared = jnp.dot(jnp.asarray(shear_mat, jnp.float32), offeq, precision=lax.Precision.HIGHEST)
    post = flat - relaxed - rate.reshape(-1) * sheared
    return post.astype(jnp.bfloat16).reshape(pops.shape)

def crop(array):
    return array[..., 1:-1, 1:-1, :]

def diff_z(array):
    return 0.5 * (array[..., 2:, 1:-1, :] - array[..., :-2, 1:-1, :])

def diff_y(array):
    return 0.5 * (array[..., 1:-1, 2:, :] - array[..., 1:-1, :-2, :])

def diff_x(array):
    return crop(0.5 * (jnp.roll(array, -1, -1) - jnp.roll(array, 1, -1)))

def smooth(array):
    first = 0.25 * (array[..., :-2, :, :] + 2.0 * array[..., 1:-1, :, :] + array[..., 2:, :, :])
    second = 0.25 * (first[..., :-2, :] + 2.0 * first[..., 1:-1, :] + first[..., 2:, :])
    return 0.25 * (jnp.roll(second, 1, -1) + 2.0 * second + jnp.roll(second, -1, -1))

def strain(field):
    grad_x, grad_y, grad_z = (diff_x(field), diff_y(field), diff_z(field))
    parts = jnp.stack([grad_x[0], grad_y[1], grad_z[2], 0.5 * (grad_y[0] + grad_x[1]), 0.5 * (grad_z[0] + grad_x[2]), 0.5 * (grad_z[1] + grad_y[2])])
    magnitude = jnp.sqrt(2.0 * (lax.optimization_barrier(jnp.sum(parts[:3] ** 2, axis=0)) + 2.0 * lax.optimization_barrier(jnp.sum(parts[3:] ** 2, axis=0))))
    return (parts, magnitude)

def pair_products(field):
    return jnp.stack([field[0] * field[0], field[1] * field[1], field[2] * field[2], field[0] * field[1], field[0] * field[2], field[1] * field[2]])

def germano(padded):
    strain_one, mag_one = strain(padded)
    hat_ss = smooth(mag_one * strain_one)
    vel_hat = smooth(padded)
    strain_hat, mag_hat = strain(vel_hat)
    hat_prods = smooth(pair_products(crop(padded)))
    leonard = hat_prods - pair_products(crop(vel_hat))
    model = 2.0 * (hat_ss - 4.0 * mag_hat * strain_hat)
    counts = jnp.asarray([1.0, 1.0, 1.0, 2.0, 2.0, 2.0], jnp.float32)[:, None, None, None]
    plane_lm = lax.optimization_barrier(jnp.sum(counts * leonard * model, axis=(0, 1)))
    plane_mm = lax.optimization_barrier(jnp.sum(counts * model * model, axis=(0, 1)))
    return (plane_lm, plane_mm, crop(mag_one))

def reference(populations, cell_index, marker_weight, segment_id):
    velocities, weights = lattice_tables()
    density, velocity = moments(populations)
    field = velocity.reshape(3, NZ, NY, CX)
    padded = jnp.concatenate([field[:, -2:], field, field[:, :2]], axis=1)
    padded = jnp.concatenate([padded[:, :, -2:], padded, padded[:, :, :2]], axis=2)

    def slab_terms(index):
        return germano(lax.dynamic_slice_in_dim(padded, index * CZ, CZ + 4, 1))
    plane_lm, plane_mm, magnitude = lax.map(slab_terms, jnp.arange(N_SPAN, dtype=jnp.int32))
    eddy_coeff = jnp.maximum(lax.optimization_barrier(jnp.sum(plane_lm, axis=0)) / (lax.optimization_barrier(jnp.sum(plane_mm, axis=0)) + eps_sum), 0.0)
    rate = 1.0 / (0.5 + 3.0 * (base_visc + eddy_coeff * magnitude.reshape(NZ, NY, CX)))
    density_grid = density.reshape(NZ, NY, CX)

    def slab_collide(index):
        start = index * CZ
        pops = lax.dynamic_slice_in_dim(populations, start, CZ, 1)
        slab_density = lax.dynamic_slice_in_dim(density_grid, start, CZ, 0)
        slab_velocity = lax.dynamic_slice_in_dim(field, start, CZ, 1)
        slab_rate = lax.dynamic_slice_in_dim(rate, start, CZ, 0)
        return collide(pops, slab_density.reshape(-1), slab_velocity.reshape(3, -1), slab_rate)
    post = lax.map(slab_collide, jnp.arange(N_SPAN, dtype=jnp.int32))
    post = jnp.moveaxis(post, 0, 1).reshape(Q, NZ, NY, CX)
    planes = []
    for index in range(19):
        shift_x, shift_y, shift_z = (velocities[index][0], velocities[index][1], velocities[index][2])
        planes.append(jnp.roll(post[index], (shift_z, shift_y, shift_x), axis=(0, 1, 2)))
    populations_next = jnp.stack(planes)
    momentum = jnp.dot(jnp.asarray(moment_basis()[1:], jnp.bfloat16), populations_next.reshape(19, -1), preferred_element_type=jnp.float32)
    marker = jnp.arange(MARKERS, dtype=jnp.int32)
    device = marker // MK_DEV
    span_pos = device // N_CROSS
    cross_pos = device % N_CROSS
    local_z = cell_index // (CY * CX)
    local_y = cell_index // CX % CY
    local_x = cell_index % CX
    global_cell = ((span_pos[:, None] * CZ + local_z) * NY + cross_pos[:, None] * CY + local_y) * CX + local_x
    picked = momentum[:, global_cell]
    force = -lax.optimization_barrier(jnp.sum(marker_weight * picked, axis=-1))
    segment_force = jax.ops.segment_sum(force.T, segment_id, num_segments=SEGMENTS).T
    return (populations_next, eddy_coeff, segment_force)
```

```python
import functools

import jax
import jax.numpy as jnp
from jax import lax
from jax.experimental import pallas as pl
from jax.experimental.pallas import tpu as pltpu
from jax.sharding import PartitionSpec as P

SEG_DEV = 8
MESH = pl.DeviceIdType.MESH
eps_sum = 1e-06
base_visc = 0.005

CHIPS_X = 4
CORES = 2

VELOCITIES = [
    (0, 0, 0),
    (1, 0, 0),
    (-1, 0, 0),
    (0, 1, 0),
    (0, -1, 0),
    (0, 0, 1),
    (0, 0, -1),
    (1, 1, 0),
    (-1, -1, 0),
    (1, -1, 0),
    (-1, 1, 0),
    (1, 0, 1),
    (-1, 0, -1),
    (1, 0, -1),
    (-1, 0, 1),
    (0, 1, 1),
    (0, -1, -1),
    (0, 1, -1),
    (0, -1, 1),
]
ORDER = [18, 5, 11, 14, 15, 3, 7, 10, 17, 6, 12, 13, 16, 4, 8, 9, 0, 1, 2]
PLACE = [ORDER.index(q) for q in range(19)]

ROW = 8
TOP = 48


def add_pairs(f):
    s = [f[2 * i + 1] + f[2 * i + 2] for i in range(9)]
    d = [f[2 * i + 1] - f[2 * i + 2] for i in range(9)]
    return s, d


def tri(low, mid, high):
    return (low + high) + (mid + mid)


def roll_x(a, shift):
    return pltpu.roll(a, shift % a.shape[-1], axis=a.ndim - 1)


def smooth_x(a):
    b = a + roll_x(a, 1)
    return b + roll_x(b, -1)


def strain_of(d):
    exy, exz, eyz = d[0][1] + d[1][0], d[0][2] + d[2][0], d[1][2] + d[2][1]
    diag = d[0][0] * d[0][0] + d[1][1] * d[1][1] + d[2][2] * d[2][2]
    off = exy * exy + exz * exz + eyz * eyz
    mag = jnp.sqrt(0.5 * diag + 0.25 * off)
    return (d[0][0], d[1][1], d[2][2], exy, exz, eyz), mag


PAIRS = [(0, 0), (1, 1), (2, 2), (0, 1), (0, 2), (1, 2)]


def kernel(
    split,
    pops_hbm,
    cell_ref,
    weight_ref,
    seg_ref,
    out_hbm,
    eddy_ref,
    force_ref,
    pops,
    vel,
    mags,
    tmp,
    vtmp,
    vhat,
    filt,
    sums,
    part,
    shear,
    post,
    outv,
    mom,
    pick,
    lanes,
    gath,
    d1s,
    d1r,
    d2,
    d3,
    h1s,
    h1r,
    h2,
    in_sem,
    out_sem,
    v_send,
    v_recv,
    p_send,
    p_recv,
    d1_send,
    d1_recv,
    d2_send,
    d2_recv,
    d3_send,
    d3_recv,
    h1_send,
    h1_recv,
    h2_send,
    h2_recv,
):
    nz, nx, nc, ny = split
    nxc = nx * nc
    nspan = nz * nxc
    cz, cy, cx = pops.shape[1:]
    half = nx // 2
    ng1, ng2 = nz * half, 2 * nc * ny
    s = lax.axis_index("span")
    y = lax.axis_index("cross")
    z, xc = s // nxc, s % nxc
    x, c = xc // nc, xc % nc
    g1 = z * half + x // 2
    g2 = (x % 2) * (nc * ny) + c * ny + y

    def xc_dev(j):
        return (z * nxc + j, y)

    def z_dev(j):
        return (j * nxc + xc, y)

    def g1_dev(j):
        return ((j // half) * nxc + ((j % half) * 2 + x % 2) * nc + c, y)

    def g2_dev(j):
        return (z * nxc + ((x // 2) * 2 + j // (nc * ny)) * nc + (j // ny) % nc, j % ny)

    def near(dz, dy):
        return ((s + dz + nspan) % nspan, (y + dy + ny) % ny)

    sides = [(1, 0), (-1, 0), (0, 1), (0, -1), (1, 1), (1, -1), (-1, 1), (-1, -1)]

    nchunk = in_sem.shape[0]
    step = cz // nchunk

    def fetch(i):
        return pltpu.make_async_copy(
            pops_hbm.at[:, pl.ds(i * step, step)], pops.at[:, pl.ds(i * step, step)], in_sem.at[i]
        )

    for i in range(nchunk):
        fetch(i).start()

    barrier = pltpu.get_barrier_semaphore()

    def greet(dev):
        pl.semaphore_signal(barrier, inc=1, device_id=dev, device_id_type=MESH)

    for dz, dy in sides:
        greet(near(dz, dy))

    def greet_group(me, count, dev):
        def body(k, carry):
            greet(dev((me + k) % count))
            return carry

        lax.fori_loop(1, count, body, 0)

    greet_group(xc, nxc, xc_dev)
    greet_group(z, nz, z_dev)
    greet_group(g1, ng1, g1_dev)
    greet_group(g2, ng2, g2_dev)
    greeted = len(sides) + (nxc - 1) + (nz - 1) + (ng1 - 1) + (ng2 - 1)

    def moments_plane(i, carry):
        f = [pops[q, i].astype(jnp.float32) for q in range(19)]
        sm, d = add_pairs(f)
        density = f[0] + ((sm[0] + sm[1] + sm[2]) + (sm[3] + sm[4] + sm[5]) + (sm[6] + sm[7] + sm[8]))
        jx = d[0] + (d[3] + d[4]) + (d[5] + d[6])
        jy = d[1] + (d[3] - d[4]) + (d[7] + d[8])
        jz = d[2] + (d[5] - d[6]) + (d[7] - d[8])
        inv = 1.0 / density
        inner = pl.ds(ROW, cy)
        vel[0, i + 2, inner, :] = jx * inv
        vel[1, i + 2, inner, :] = jy * inv
        vel[2, i + 2, inner, :] = jz * inv
        return carry

    for i in range(nchunk):
        fetch(i).wait()
        lax.fori_loop(i * step, (i + 1) * step, moments_plane, 0)

    pl.semaphore_wait(barrier, greeted)

    def span_of(d, size, width):
        first = size[0]
        if d == 0:
            return pl.ds(first, size[1]), pl.ds(first, size[1])
        if d > 0:
            return pl.ds(first + size[1] - width, width), pl.ds(first - width, width)
        return pl.ds(first, width), pl.ds(first + size[1], width)

    def vel_copy(i):
        dz, dy = sides[i]
        zs, zt = span_of(dz, (2, cz), 2)
        ys, yt = span_of(dy, (ROW, cy), 2)
        return pltpu.make_async_remote_copy(
            src_ref=vel.at[:, zs, ys, :],
            dst_ref=vel.at[:, zt, yt, :],
            send_sem=v_send.at[i],
            recv_sem=v_recv.at[i],
            device_id=near(dz, dy),
            device_id_type=MESH,
        )

    for i in range(len(sides)):
        vel_copy(i).start()

    nmark, kk = cell_ref.shape
    nrows = cz * cy
    row_iota = lax.broadcasted_iota(jnp.int32, (nmark, nrows), 1)
    lane_iota = lax.broadcasted_iota(jnp.int32, (nmark, cx), 1)
    cells = cell_ref[...]
    weights = weight_ref[...]
    for k in range(kk):
        cell = cells[:, k : k + 1]
        line = cell // cx
        pick[k * nmark : (k + 1) * nmark, :] = jnp.where(row_iota == line, 1.0, 0.0).astype(
            jnp.bfloat16
        )
        lanes[k * nmark : (k + 1) * nmark, :] = jnp.where(
            lane_iota == cell - line * cx, weights[:, k : k + 1], 0.0
        )

    for i in range(len(sides)):
        vel_copy(i).wait_recv()

    def first_pass(i, carry):
        mid, low, high = pl.ds(ROW - 1, 40), pl.ds(ROW - 2, 40), pl.ds(ROW, 40)
        v = [vel[a, i + 1, mid, :] for a in range(3)]
        d = []
        for a in range(3):
            dx = roll_x(v[a], -1) - roll_x(v[a], 1)
            dy = vel[a, i + 1, high, :] - vel[a, i + 1, low, :]
            dz = vel[a, i + 2, mid, :] - vel[a, i, mid, :]
            d.append((dx, dy, dz))
        e, mag = strain_of(d)
        mags[i] = mag
        half_mag = 0.5 * mag
        for n in range(3):
            tmp[n] = smooth_x(mag * e[n])
            tmp[n + 3] = smooth_x(half_mag * e[n + 3])
        for n, (a, b) in enumerate(PAIRS):
            tmp[n + 6] = smooth_x(v[a] * v[b])
        for n in range(12):
            filt[n, i] = tri(tmp[n, 0:cy, :], tmp[n, 1 : cy + 1, :], tmp[n, 2 : cy + 2, :])
        for a in range(3):
            along_z = tri(vel[a, i, low, :], vel[a, i + 1, low, :], vel[a, i + 2, low, :])
            vtmp[a, 0:40, :] = smooth_x(along_z)
        for a in range(3):
            vhat[a, i] = (1.0 / 64.0) * tri(vtmp[a, 0:40, :], vtmp[a, 1:41, :], vtmp[a, 2:42, :])
        return carry

    lax.fori_loop(0, cz + 2, first_pass, 0)

    def second_pass(i, carry):
        plane_lm, plane_mm = carry
        mid, low, high = pl.ds(1, cy), pl.ds(0, cy), pl.ds(2, cy)
        v = [vhat[a, i + 1, mid, :] for a in range(3)]
        d = []
        for a in range(3):
            dx = roll_x(v[a], -1) - roll_x(v[a], 1)
            dy = vhat[a, i + 1, high, :] - vhat[a, i + 1, low, :]
            dz = vhat[a, i + 2, mid, :] - vhat[a, i, mid, :]
            d.append((dx, dy, dz))
        e, mag = strain_of(d)
        four, two = 4.0 * mag, 2.0 * mag
        lm = mm = lm_off = mm_off = None
        for n, (a, b) in enumerate(PAIRS):
            hat_ss = tri(filt[n, i], filt[n, i + 1], filt[n, i + 2])
            hat_vv = tri(filt[n + 6, i], filt[n + 6, i + 1], filt[n + 6, i + 2])
            model = (1.0 / 64.0) * hat_ss - (four if n < 3 else two) * e[n]
            leonard = (1.0 / 64.0) * hat_vv - v[a] * v[b]
            if n == 0:
                lm, mm = leonard * model, model * model
            elif n < 3:
                lm, mm = lm + leonard * model, mm + model * model
            elif n == 3:
                lm_off, mm_off = leonard * model, model * model
            else:
                lm_off, mm_off = lm_off + leonard * model, mm_off + model * model
        return plane_lm + (lm + 2.0 * lm_off), plane_mm + (mm + 2.0 * mm_off)

    zero = jnp.zeros((cy, cx), jnp.float32)
    plane_lm, plane_mm = lax.fori_loop(0, cz, second_pass, (zero, zero))

    rows = cy // nxc
    sums[0] = plane_lm
    sums[1] = plane_mm
    for j in range(nxc):
        d1s[j, 0:rows, :] = sums[0, j * rows : (j + 1) * rows, :]
        d1s[j, rows : 2 * rows, :] = sums[1, j * rows : (j + 1) * rows, :]

    def exchange(src, dst, slot, send, recv, dev, j):
        return pltpu.make_async_remote_copy(
            src_ref=src,
            dst_ref=dst.at[slot],
            send_sem=send.at[j],
            recv_sem=recv.at[slot],
            device_id=dev(j),
            device_id_type=MESH,
        )

    def for_others(me, count, act):
        def body(k, carry):
            act((me + k) % count)
            return carry

        lax.fori_loop(1, count, body, 0)

    def d1_send_to(j):
        exchange(d1s.at[j], d1r, xc, d1_send, d1_recv, xc_dev, j).start()

    def d1_from(j):
        exchange(d1s.at[j], d1r, j, d1_send, d1_recv, xc_dev, j).wait_recv()

    def d2_send_to(j):
        exchange(d2.at[z], d2, z, d2_send, d2_recv, z_dev, j).start()

    def d2_from(j):
        exchange(d2.at[z], d2, j, d2_send, d2_recv, z_dev, j).wait_recv()

    def d3_send_to(j):
        exchange(d3.at[xc], d3, xc, d3_send, d3_recv, xc_dev, j).start()

    def d3_from(j):
        exchange(d3.at[xc], d3, j, d3_send, d3_recv, xc_dev, j).wait_recv()

    def collide_plane(i, carry):
        inner = pl.ds(ROW, cy)
        f = [pops[q, i].astype(jnp.float32) for q in range(19)]
        sm, d = add_pairs(f)
        sx, sy, sz, sa, sb, sc, sd, se, sg = sm
        dx, dy, dz, da, db, dc, dd, de, dg = d
        ux, uy, uz = [vel[a, i + 2, inner, :] for a in range(3)]
        xy, xz, yz = sa + sb, sc + sd, se + sg
        axis, diag = sx + sy + sz, xy + xz + yz
        abp, abm, cdp, cdm, egp, egm = da + db, da - db, dc + dd, dc - dd, de + dg, de - dg
        jx, jy, jz = dx + (abp + cdp), dy + (abm + egp), dz + (cdm + egm)
        jxx, jyy, jzz = jx * ux, jy * uy, jz * uz
        ju = jxx + jyy + jzz
        ne = (1.19 * 19.0 / 2394.0) * (diag - f[0] - ju)
        neps = (1.4 / 252.0) * (9.0 * f[0] - 7.0 * axis - 2.0 * diag + 5.5 * ju)
        ax_part = -11.0 * ne - 4.0 * neps
        dg_part = 8.0 * ne + neps
        eq_xx = 3.0 * jxx - ju
        eq_ww = jyy - jzz
        axis_xx, diag_xx = 3.0 * sx - axis, diag - 3.0 * yz
        axis_ww, diag_ww = sy - sz, xy - xz
        pi_xx = (1.4 / 72.0) * (diag_xx - 2.0 * axis_xx + 0.5 * eq_xx)
        pi_ww = (1.4 / 24.0) * (diag_ww - 2.0 * axis_ww + 0.5 * eq_ww)
        shear[0, i] = (1.0 / 36.0) * (axis_xx + diag_xx - eq_xx)
        shear[1, i] = (1.0 / 12.0) * (axis_ww + diag_ww - eq_ww)
        shear[2, i] = 0.25 * (sa - sb - jx * uy)
        shear[3, i] = 0.25 * (sc - sd - jx * uz)
        shear[4, i] = 0.25 * (se - sg - jy * uz)
        two_xx, two_ww = 2.0 * pi_xx, 2.0 * pi_ww
        base_yz = ax_part + two_xx
        hx = ax_part - 2.0 * two_xx
        hy, hz = base_yz - two_ww, base_yz + two_ww
        base_d = dg_part + pi_xx
        hxy, hxz, hyz = base_d + pi_ww, base_d - pi_ww, dg_part - two_xx
        tx = (1.2 / 8.0) * ((1.0 / 3.0) * jx - dx)
        ty = (1.2 / 8.0) * ((1.0 / 3.0) * jy - dy)
        tz = (1.2 / 8.0) * ((1.0 / 3.0) * jz - dz)
        mx = (1.98 / 8.0) * (abp - cdp)
        my = (1.98 / 8.0) * (egp - abm)
        mz = (1.98 / 8.0) * (cdm - egm)
        xp, xm, yp, ym, zp, zm = tx + mx, tx - mx, ty + my, ty - my, tz + mz, tz - mz
        halves = [
            (hx, -4.0 * tx),
            (hy, -4.0 * ty),
            (hz, -4.0 * tz),
            (hxy, xp + ym),
            (hxy, xp - ym),
            (hxz, xm + zp),
            (hxz, xm - zp),
            (hyz, yp + zm),
            (hyz, yp - zm),
        ]
        part[0, i] = f[0] + (30.0 * ne - 12.0 * neps)
        for n, (even, odd) in enumerate(halves):
            part[2 * n + 1, i] = f[2 * n + 1] - (even + odd)
            part[2 * n + 2, i] = f[2 * n + 2] - (even - odd)
        return carry

    third = (cz + 2) // 3

    for_others(xc, nxc, d1_send_to)
    d1r[xc] = d1s[xc]
    lax.fori_loop(0, third, collide_plane, 0)
    for_others(xc, nxc, d1_from)
    total = d1r[0]
    for j in range(1, nxc):
        total = total + d1r[j]
    d2[z] = total
    for_others(z, nz, d2_send_to)
    lax.fori_loop(third, 2 * third, collide_plane, 0)
    for_others(z, nz, d2_from)
    total = d2[0]
    for j in range(1, nz):
        total = total + d2[j]
    d1r[0] = total
    eddy_rows = jnp.maximum(d1r[0, 0:rows, :] / (d1r[0, rows : 2 * rows, :] + eps_sum), 0.0)
    d3[xc, 0:rows, :] = eddy_rows
    d3[xc, rows : 2 * rows, :] = eddy_rows
    for_others(xc, nxc, d3_send_to)
    lax.fori_loop(2 * third, cz, collide_plane, 0)
    for_others(xc, nxc, d3_from)
    for j in range(nxc):
        eddy_ref[j * rows : (j + 1) * rows, :] = d3[j, 0:rows, :]

    def finish_plane(i, carry):
        mag = mags[i + 1, 1 : cy + 1, :]
        rate = 1.0 / (0.5 + 3.0 * (base_visc + eddy_ref[...] * mag))
        rxx, rww, rxy, rxz, ryz = [rate * shear[n, i] for n in range(5)]
        diag_y, diag_z, diag_yz = rxx + rww, rxx - rww, -2.0 * rxx
        lost = [
            2.0 * rxx,
            rww - rxx,
            -diag_y,
            diag_y + rxy,
            diag_y - rxy,
            diag_z + rxz,
            diag_z - rxz,
            diag_yz + ryz,
            diag_yz - ryz,
        ]
        inner = pl.ds(ROW, cy)

        def keep(q, value):
            post[PLACE[q], i + 1, inner, :] = value.astype(jnp.bfloat16).astype(jnp.float32)

        keep(0, part[0, i])
        for n in range(9):
            keep(2 * n + 1, part[2 * n + 1, i] - lost[n])
            keep(2 * n + 2, part[2 * n + 2, i] - lost[n])
        return carry

    lax.fori_loop(0, cz, finish_plane, 0)

    crossing = [
        ((1, 0), 0, 5),
        ((-1, 0), 8, 5),
        ((0, 1), 4, 5),
        ((0, -1), 12, 4),
        ((0, -1), 0, 1),
        ((1, 1), 4, 1),
        ((1, -1), 0, 1),
        ((-1, 1), 8, 1),
        ((-1, -1), 12, 1),
    ]

    def post_copy(i):
        (dz, dy), first, count = crossing[i]
        zs, zt = span_of(dz, (1, cz), 1)
        ys, yt = span_of(dy, (ROW, cy), 1)
        group = pl.ds(first, count)
        return pltpu.make_async_remote_copy(
            src_ref=post.at[group, zs, ys, :],
            dst_ref=post.at[group, zt, yt, :],
            send_sem=p_send.at[i],
            recv_sem=p_recv.at[i],
            device_id=near(dz, dy),
            device_id_type=MESH,
        )

    for i in range(len(crossing)):
        post_copy(i).start()
    for i in range(len(crossing)):
        post_copy(i).wait_recv()

    def put(i):
        return pltpu.make_async_copy(outv.at[:, i], out_hbm.at[:, i], out_sem.at[i])

    def stream_plane(i, carry):
        f = []
        for q, (ex, ey, ez) in enumerate(VELOCITIES):
            value = post[PLACE[q], i + 1 - ez, pl.ds(ROW - ey, cy), :]
            if ex:
                value = roll_x(value, ex)
            outv[q, i] = value.astype(jnp.bfloat16)
            f.append(value)
        put(i).start()
        d = [f[2 * n + 1] - f[2 * n + 2] for n in range(9)]
        jx = d[0] + (d[3] + d[4]) + (d[5] + d[6])
        jy = d[1] + (d[3] - d[4]) + (d[7] + d[8])
        jz = d[2] + (d[5] - d[6]) + (d[7] - d[8])
        lines = pl.ds(pl.multiple_of(i * cy, cy), cy)
        for n, value in enumerate((jx, jy, jz)):
            high = value.astype(jnp.bfloat16)
            low = (value - high.astype(jnp.float32)).astype(jnp.bfloat16)
            mom[lines, 2 * n * cx : (2 * n + 1) * cx] = high
            mom[lines, (2 * n + 1) * cx : (2 * n + 2) * cx] = low
        return carry

    lax.fori_loop(0, cz, stream_plane, 0)

    gath[...] = jnp.dot(pick[...], mom[...], preferred_element_type=jnp.float32)
    forces = []
    ones = jnp.ones((8, cx), jnp.bfloat16)

    def parts_of(value):
        first = value.astype(jnp.bfloat16)
        rest = value - first.astype(jnp.float32)
        second = rest.astype(jnp.bfloat16)
        third_part = (rest - second.astype(jnp.float32)).astype(jnp.bfloat16)
        return first, second, third_part

    def dot_t(a, b):
        return lax.dot_general(a, b, (((1,), (1,)), ((), ())), preferred_element_type=jnp.float32)

    for n in range(3):
        acc = None
        for k in range(kk):
            block = pl.ds(k * nmark, nmark)
            both = (
                gath[block, 2 * n * cx : (2 * n + 1) * cx]
                + gath[block, (2 * n + 1) * cx : (2 * n + 2) * cx]
            )
            term = lanes[block, :] * both
            acc = term if acc is None else acc + term
        a, b, e = parts_of(acc)
        forces.append(-(dot_t(ones, a) + dot_t(ones, b) + dot_t(ones, e)))
    which = lax.broadcasted_iota(jnp.int32, (8, nmark), 0)
    force = jnp.where(which == 0, forces[0], jnp.where(which == 1, forces[1], forces[2]))
    a, b, e = parts_of(force)
    ids = seg_ref[...].reshape(1, nmark)
    lane_count = SEG_DEV * ng2
    seg_iota = lax.broadcasted_iota(jnp.int32, (lane_count, nmark), 0)
    for j in range(ng1):
        hot = jnp.where(seg_iota == ids - j * lane_count, 1.0, 0.0).astype(jnp.bfloat16)
        h1s[j] = dot_t(a, hot) + dot_t(b, hot) + dot_t(e, hot)

    def h1_send_to(j):
        exchange(h1s.at[j], h1r, g1, h1_send, h1_recv, g1_dev, j).start()

    def h1_from(j):
        exchange(h1s.at[j], h1r, j, h1_send, h1_recv, g1_dev, j).wait_recv()

    def h2_send_to(j):
        exchange(h2.at[g2], h2, g2, h2_send, h2_recv, g2_dev, j).start()

    def h2_from(j):
        exchange(h2.at[g2], h2, j, h2_send, h2_recv, g2_dev, j).wait_recv()

    for_others(g1, ng1, h1_send_to)
    h1r[g1] = h1s[g1]
    for_others(g1, ng1, h1_from)
    total = h1r[0]
    for j in range(1, ng1):
        total = total + h1r[j]
    h2[g2] = total
    for_others(g2, ng2, h2_send_to)
    for_others(g2, ng2, h2_from)
    total = h2[0]
    for j in range(1, ng2):
        total = total + h2[j]
    mine = pltpu.roll(total, (lane_count - g2 * SEG_DEV) % lane_count, axis=1)
    force_ref[...] = mine[0:3, 0:SEG_DEV]

    for i in range(len(sides)):
        vel_copy(i).wait_send()
    for i in range(len(crossing)):
        post_copy(i).wait_send()

    def d1_sent(j):
        exchange(d1s.at[j], d1r, xc, d1_send, d1_recv, xc_dev, j).wait_send()

    def d2_sent(j):
        exchange(d2.at[z], d2, z, d2_send, d2_recv, z_dev, j).wait_send()

    def d3_sent(j):
        exchange(d3.at[xc], d3, xc, d3_send, d3_recv, xc_dev, j).wait_send()

    def h1_sent(j):
        exchange(h1s.at[j], h1r, g1, h1_send, h1_recv, g1_dev, j).wait_send()

    def h2_sent(j):
        exchange(h2.at[g2], h2, g2, h2_send, h2_recv, g2_dev, j).wait_send()

    for_others(xc, nxc, d1_sent)
    for_others(z, nz, d2_sent)
    for_others(xc, nxc, d3_sent)
    for_others(g1, ng1, h1_sent)
    for_others(g2, ng2, h2_sent)

    def put_done(i, carry):
        put(i).wait()
        return carry

    lax.fori_loop(0, cz, put_done, 0)


def local(split, populations, cell_index, marker_weight, segment_id):
    nq, cz, cy, cx = populations.shape
    nmark, kk = cell_index.shape
    nz, nx, nc, ny = split
    nxc = nx * nc
    ng1, ng2 = nz * (nx // 2), 2 * nc * ny
    rows = cy // nxc
    f32, bf16 = jnp.float32, jnp.bfloat16
    dma = pltpu.SemaphoreType.DMA
    vmem = pl.BlockSpec(memory_space=pltpu.VMEM)
    hbm = pl.BlockSpec(memory_space=pl.ANY)
    lane_count = SEG_DEV * ng2
    scratch = [
        pltpu.VMEM((nq, cz, cy, cx), bf16),
        pltpu.VMEM((3, cz + 4, TOP, cx), f32),
        pltpu.VMEM((cz + 2, 40, cx), f32),
        pltpu.VMEM((12, 40, cx), f32),
        pltpu.VMEM((3, 48, cx), f32),
        pltpu.VMEM((3, cz + 2, 40, cx), f32),
        pltpu.VMEM((12, cz + 2, cy, cx), f32),
        pltpu.VMEM((2, cy, cx), f32),
        pltpu.VMEM((nq, cz, cy, cx), f32),
        pltpu.VMEM((5, cz, cy, cx), f32),
        pltpu.VMEM((nq, cz + 2, TOP, cx), f32),
        pltpu.VMEM((nq, cz, cy, cx), bf16),
        pltpu.VMEM((cz * cy, 6 * cx), bf16),
        pltpu.VMEM((kk * nmark, cz * cy), bf16),
        pltpu.VMEM((kk * nmark, cx), f32),
        pltpu.VMEM((kk * nmark, 6 * cx), f32),
        pltpu.VMEM((nxc, 2 * rows, cx), f32),
        pltpu.VMEM((nxc, 2 * rows, cx), f32),
        pltpu.VMEM((nz, 2 * rows, cx), f32),
        pltpu.VMEM((nxc, 2 * rows, cx), f32),
        pltpu.VMEM((ng1, 8, lane_count), f32),
        pltpu.VMEM((ng1, 8, lane_count), f32),
        pltpu.VMEM((ng2, 8, lane_count), f32),
        dma((4,)),
        dma((cz,)),
        dma((8,)),
        dma((8,)),
        dma((9,)),
        dma((9,)),
        dma((nxc,)),
        dma((nxc,)),
        dma((nz,)),
        dma((nz,)),
        dma((nxc,)),
        dma((nxc,)),
        dma((ng1,)),
        dma((ng1,)),
        dma((ng2,)),
        dma((ng2,)),
    ]
    return pl.pallas_call(
        functools.partial(kernel, split),
        out_shape=(
            jax.ShapeDtypeStruct((nq, cz, cy, cx), bf16),
            jax.ShapeDtypeStruct((cy, cx), f32),
            jax.ShapeDtypeStruct((3, SEG_DEV), f32),
        ),
        in_specs=[hbm, vmem, vmem, vmem],
        out_specs=(hbm, vmem, vmem),
        scratch_shapes=scratch,
        compiler_params=pltpu.CompilerParams(
            collective_id=0, has_side_effects=True, vmem_limit_bytes=50 * 1024 * 1024
        ),
    )(populations, cell_index, marker_weight, segment_id)


def solution(mesh):
    in_specs = (
        P(None, "span", "cross", None),
        P(("span", "cross"), None),
        P(("span", "cross"), None),
        P(("span", "cross")),
    )
    out_specs = (P(None, "span", "cross", None), P("cross", None), P(None, ("span", "cross")))
    sizes = dict(mesh.shape)
    split = (sizes["span"] // (CHIPS_X * CORES), CHIPS_X, CORES, sizes["cross"])
    return jax.shard_map(
        functools.partial(local, split),
        mesh=mesh,
        in_specs=in_specs,
        out_specs=out_specs,
        check_vma=False,
    )
```

```python
import functools

import jax
import jax.numpy as jnp
from jax import lax
from jax.experimental import pallas as pl
from jax.experimental.pallas import tpu as pltpu
from jax.sharding import PartitionSpec as P

SEG_DEV = 8
MESH = pl.DeviceIdType.MESH
eps_sum = 1e-06
base_visc = 0.005

CHIPS_X = 4
CORES = 2

VELOCITIES = [
    (0, 0, 0),
    (1, 0, 0),
    (-1, 0, 0),
    (0, 1, 0),
    (0, -1, 0),
    (0, 0, 1),
    (0, 0, -1),
    (1, 1, 0),
    (-1, -1, 0),
    (1, -1, 0),
    (-1, 1, 0),
    (1, 0, 1),
    (-1, 0, -1),
    (1, 0, -1),
    (-1, 0, 1),
    (0, 1, 1),
    (0, -1, -1),
    (0, 1, -1),
    (0, -1, 1),
]
ORDER = [18, 5, 11, 14, 15, 3, 7, 10, 17, 6, 12, 13, 16, 4, 8, 9, 0, 1, 2]
PLACE = [ORDER.index(q) for q in range(19)]

ROW = 8
TOP = 48


def add_pairs(f):
    s = [f[2 * i + 1] + f[2 * i + 2] for i in range(9)]
    d = [f[2 * i + 1] - f[2 * i + 2] for i in range(9)]
    return s, d


def tri(low, mid, high):
    return (low + high) + (mid + mid)


def roll_x(a, shift):
    return pltpu.roll(a, shift % a.shape[-1], axis=a.ndim - 1)


def strain_of(d):
    exy, exz, eyz = d[0][1] + d[1][0], d[0][2] + d[2][0], d[1][2] + d[2][1]
    diag = d[0][0] * d[0][0] + d[1][1] * d[1][1] + d[2][2] * d[2][2]
    off = exy * exy + exz * exz + eyz * eyz
    mag = jnp.sqrt(0.5 * diag + 0.25 * off)
    return (d[0][0], d[1][1], d[2][2], exy, exz, eyz), mag


PAIRS = [(0, 0), (1, 1), (2, 2), (0, 1), (0, 2), (1, 2)]


SIDES = [(1, 0), (-1, 0), (0, 1), (0, -1), (1, 1), (1, -1), (-1, 1), (-1, -1)]
XZ, XX, WW, YZ, XY = range(5)


def near(split, dz, dy):
    nz, nx, nc, ny = split
    nspan = nz * nx * nc
    s, y = lax.axis_index("span"), lax.axis_index("cross")
    return ((s + dz + nspan) % nspan, (y + dy + ny) % ny)


def ranges(d, first, size, width):
    if d == 0:
        return pl.ds(first, size), pl.ds(first, size)
    if d > 0:
        return pl.ds(first + size - width, width), pl.ds(first - width, width)
    return pl.ds(first, width), pl.ds(first + size, width)


def velocity_kernel(split, pops_hbm, vel, pops, in_sem, v_send, v_recv):
    cz, cy, cx = pops.shape[1:]
    nchunk = in_sem.shape[0]
    step = cz // nchunk

    def fetch(i):
        some = pl.ds(i * step, step)
        return pltpu.make_async_copy(pops_hbm.at[:, some], pops.at[:, some], in_sem.at[i])

    for i in range(nchunk):
        fetch(i).start()
    barrier = pltpu.get_barrier_semaphore()
    for dz, dy in SIDES:
        pl.semaphore_signal(
            barrier, inc=1, device_id=near(split, dz, dy), device_id_type=MESH
        )

    def moments_plane(i, carry):
        f = [pops[q, i].astype(jnp.float32) for q in range(19)]
        sm, d = add_pairs(f)
        density = f[0] + ((sm[0] + sm[1] + sm[2]) + (sm[3] + sm[4] + sm[5]) + (sm[6] + sm[7] + sm[8]))
        jx = d[0] + (d[3] + d[4]) + (d[5] + d[6])
        jy = d[1] + (d[3] - d[4]) + (d[7] + d[8])
        jz = d[2] + (d[5] - d[6]) + (d[7] - d[8])
        inv = 1.0 / density
        inner = pl.ds(ROW, cy)
        vel[0, i + 2, inner, :] = jx * inv
        vel[1, i + 2, inner, :] = jy * inv
        vel[2, i + 2, inner, :] = jz * inv
        return carry

    for i in range(nchunk):
        fetch(i).wait()
        lax.fori_loop(i * step, (i + 1) * step, moments_plane, 0)

    pl.semaphore_wait(barrier, len(SIDES))

    def vel_copy(i):
        dz, dy = SIDES[i]
        zs, zt = ranges(dz, 2, cz, 2)
        ys, yt = ranges(dy, ROW, cy, 2)
        return pltpu.make_async_remote_copy(
            src_ref=vel.at[:, zs, ys, :],
            dst_ref=vel.at[:, zt, yt, :],
            send_sem=v_send.at[i],
            recv_sem=v_recv.at[i],
            device_id=near(split, dz, dy),
            device_id_type=MESH,
        )

    for i in range(len(SIDES)):
        vel_copy(i).start()
    for i in range(len(SIDES)):
        vel_copy(i).wait()


def step_kernel(
    split,
    vel,
    pops,
    cell_ref,
    weight_ref,
    seg_ref,
    outv,
    eddy_ref,
    force_ref,
    smoother,
    hats_a,
    hats_b,
    mags,
    tmp_a,
    tmp_b,
    vtmp_a,
    vtmp_b,
    vhat,
    filt,
    sums,
    shear,
    post,
    eddyx,
    mom,
    pick,
    lanes,
    gath,
    hot,
    d1s,
    d1r,
    d2,
    d3,
    dlow,
    dhigh,
    h1s,
    h1r,
    h2,
    p_send,
    p_recv,
    s_send,
    s_recv,
    d1_send,
    d1_recv,
    d2_send,
    d2_recv,
    d3_send,
    d3_recv,
    e_send,
    e_recv,
    h1_send,
    h1_recv,
    h2_send,
    h2_recv,
):
    nz, nx, nc, ny = split
    nxc = nx * nc
    cz, cy, cx = pops.shape[1:]
    half = nx // 2
    ng1, ng2 = nz * half, 2 * nc * ny
    s = lax.axis_index("span")
    y = lax.axis_index("cross")
    z, xc = s // nxc, s % nxc
    x, c = xc // nc, xc % nc
    g1 = z * half + x // 2
    g2 = y * (2 * nc) + (x % 2) * nc + c
    place = (x % 2) * (nc * ny) + c * ny + y
    y_up, y_down = (y + 1) % ny, (y + ny - 1) % ny

    def xc_dev(j):
        return (z * nxc + j, y)

    def z_dev(j):
        return (j * nxc + xc, y)

    def g1_dev(j):
        return ((j // half) * nxc + ((j % half) * 2 + x % 2) * nc + c, y)

    def g2_dev(j):
        return (z * nxc + (x // 2) * (2 * nc) + j % (2 * nc), j // (2 * nc))

    def for_others(me, count, act, unroll=False):
        def body(t, carry):
            away = count // 2 + (t // 2) * (1 - 2 * (t % 2))
            act((me + away) % count)
            return carry

        lax.fori_loop(1, count, body, 0, unroll=unroll)

    def for_all(count, act):
        def body(j, carry):
            act(j)
            return carry

        lax.fori_loop(0, count, body, 0)

    barrier = pltpu.get_barrier_semaphore()

    def greet(dev):
        pl.semaphore_signal(barrier, inc=1, device_id=dev, device_id_type=MESH)

    for_others(g1, ng1, lambda j: greet(g1_dev(j)))
    for_others(g2, ng2, lambda j: greet(g2_dev(j)))
    for_others(z, nz, lambda j: greet(z_dev(j)))
    for_others(xc, nxc, lambda j: greet(xc_dev(j)))
    for dz, dy in SIDES:
        greet(near(split, dz, dy))
    greet((z * nxc + nxc - 1, y_down))
    greet((z * nxc, y_up))
    last, first = xc == nxc - 1, xc == 0
    greeted = len(SIDES) + (nxc - 1) + (nz - 1) + (ng1 - 1) + (ng2 - 1)
    greeted = greeted + jnp.where(jnp.logical_or(last, first), nxc, 0)

    apart = lax.broadcasted_iota(jnp.int32, (cx, cx), 0) - lax.broadcasted_iota(jnp.int32, (cx, cx), 1)
    apart = (apart + cx) % cx
    beside = jnp.logical_or(apart == 1, apart == cx - 1)
    circulant = jnp.where(apart == 0, 2.0, jnp.where(beside, 1.0, 0.0)).astype(jnp.bfloat16)
    for n in range(3):
        smoother[n * cx : (n + 1) * cx, :] = circulant

    def smooth_x(values):
        both = jnp.concatenate(values, axis=0)
        high = both.astype(jnp.bfloat16)
        rest = both - high.astype(jnp.float32)
        mid = rest.astype(jnp.bfloat16)
        low = (rest - mid.astype(jnp.float32)).astype(jnp.bfloat16)
        parts = jnp.concatenate([high, mid, low], axis=1)
        return jnp.dot(parts, smoother[...], preferred_element_type=jnp.float32)

    def products(p, tmp, vtmp):
        mid, low, high = pl.ds(ROW - 1, 40), pl.ds(ROW - 2, 40), pl.ds(ROW, 40)
        v = [vel[a, p + 1, mid, :] for a in range(3)]
        for n, (a, b) in enumerate(PAIRS):
            tmp[n + 6] = v[a] * v[b]
        d = []
        for a in range(3):
            below = vel[a, p + 1, low, :]
            vtmp[a, 0:40, :] = tri(vel[a, p, low, :], below, vel[a, p + 2, low, :])
            dx = roll_x(v[a], -1) - roll_x(v[a], 1)
            dy = vel[a, p + 1, high, :] - below
            dz = vel[a, p + 2, mid, :] - vel[a, p, mid, :]
            d.append((dx, dy, dz))
        e, mag = strain_of(d)
        mags[p] = mag
        half_mag = 0.5 * mag
        for n in range(3):
            tmp[n] = mag * e[n]
            tmp[n + 3] = half_mag * e[n + 3]

    def filters(p, tmp, vtmp):
        for n in range(12):
            filt[n, p + 1] = tri(tmp[n, 0:cy, :], tmp[n, 1 : cy + 1, :], tmp[n, 2 : cy + 2, :])
        along_y = [tri(vtmp[a, 0:40, :], vtmp[a, 1:41, :], vtmp[a, 2:42, :]) for a in range(3)]
        smoothed = smooth_x(along_y)
        for a in range(3):
            vhat[a, p + 1] = (1.0 / 64.0) * smoothed[a * 40 : (a + 1) * 40]

    def two_planes(i, carry):
        products(2 * i, tmp_a, vtmp_a)
        filters(2 * i - 1, tmp_b, vtmp_b)
        products(2 * i + 1, tmp_b, vtmp_b)
        filters(2 * i, tmp_a, vtmp_a)
        return carry

    lax.fori_loop(0, (cz + 2) // 2, two_planes, 0)
    filters(cz + 1, tmp_b, vtmp_b)

    def hats_of(i, hats):
        along_z = [tri(filt[n, i + 1], filt[n, i + 2], filt[n, i + 3]) for n in range(12)]
        smoothed = smooth_x(along_z)
        for n in range(12):
            hats[n] = (1.0 / 64.0) * smoothed[n * cy : (n + 1) * cy]

    def add_plane(i, hats, plane_lm, plane_mm):
        mid, low, high = pl.ds(1, cy), pl.ds(0, cy), pl.ds(2, cy)
        v = [vhat[a, i + 2, mid, :] for a in range(3)]
        d = []
        for a in range(3):
            dx = roll_x(v[a], -1) - roll_x(v[a], 1)
            dy = vhat[a, i + 2, high, :] - vhat[a, i + 2, low, :]
            dz = vhat[a, i + 3, mid, :] - vhat[a, i + 1, mid, :]
            d.append((dx, dy, dz))
        e, mag = strain_of(d)
        four, two = 4.0 * mag, 2.0 * mag
        lm = mm = lm_off = mm_off = None
        for n, (a, b) in enumerate(PAIRS):
            model = hats[n] - (four if n < 3 else two) * e[n]
            leonard = hats[n + 6] - v[a] * v[b]
            if n == 0:
                lm, mm = leonard * model, model * model
            elif n < 3:
                lm, mm = lm + leonard * model, mm + model * model
            elif n == 3:
                lm_off, mm_off = leonard * model, model * model
            else:
                lm_off, mm_off = lm_off + leonard * model, mm_off + model * model
        return plane_lm + (lm + 2.0 * lm_off), plane_mm + (mm + 2.0 * mm_off)

    def second_pass(i, carry):
        hats_of(2 * i + 1, hats_b)
        carry = add_plane(2 * i, hats_a, *carry)
        hats_of(2 * i + 2, hats_a)
        return add_plane(2 * i + 1, hats_b, *carry)

    zero = jnp.zeros((cy, cx), jnp.float32)
    hats_of(0, hats_a)
    plane_lm, plane_mm = lax.fori_loop(0, cz // 2, second_pass, (zero, zero))

    rows = cy // nxc
    sums[0] = plane_lm
    sums[1] = plane_mm
    for j in range(nxc):
        d1s[j, 0:rows, :] = sums[0, j * rows : (j + 1) * rows, :]
        d1s[j, rows : 2 * rows, :] = sums[1, j * rows : (j + 1) * rows, :]

    def exchange(src, dst, slot, send, recv, dev, j):
        return pltpu.make_async_remote_copy(
            src_ref=src,
            dst_ref=dst.at[slot],
            send_sem=send.at[j],
            recv_sem=recv.at[slot],
            device_id=dev(j),
            device_id_type=MESH,
        )

    def d1_copy(j, slot):
        return exchange(d1s.at[j], d1r, slot, d1_send, d1_recv, xc_dev, j)

    def d2_copy(j, slot):
        return exchange(d2.at[z], d2, slot, d2_send, d2_recv, z_dev, j)

    def d3_copy(j, slot):
        return exchange(d3.at[xc], d3, slot, d3_send, d3_recv, xc_dev, j)

    def edge_copy(j, side):
        return pltpu.make_async_remote_copy(
            src_ref=d3.at[xc],
            dst_ref=dlow if side == 0 else dhigh,
            send_sem=e_send.at[side, j],
            recv_sem=e_recv.at[side],
            device_id=(z * nxc + j, y_up if side == 0 else y_down),
            device_id_type=MESH,
        )

    def h1_copy(j, slot):
        return exchange(h1s.at[j], h1r, slot, h1_send, h1_recv, g1_dev, j)

    def h2_copy(j, slot):
        return exchange(h2.at[g2], h2, slot, h2_send, h2_recv, g2_dev, j)

    pl.semaphore_wait(barrier, greeted)
    for_others(xc, nxc, lambda j: d1_copy(j, xc).start())

    inner = pl.ds(ROW, cy)

    def collide_plane(i, carry):
        f = [pops[q, i].astype(jnp.float32) for q in range(19)]
        sm, d = add_pairs(f)
        sx, sy, sz, sa, sb, sc, sd, se, sg = sm
        dx, dy, dz, da, db, dc, dd, de, dg = d
        ux, uy, uz = [vel[a, i + 2, inner, :] for a in range(3)]
        xy, xz, yz = sa + sb, sc + sd, se + sg
        axis, diag = sx + sy + sz, xy + xz + yz
        abp, abm, cdp, cdm, egp, egm = da + db, da - db, dc + dd, dc - dd, de + dg, de - dg
        jx, jy, jz = dx + (abp + cdp), dy + (abm + egp), dz + (cdm + egm)
        jxx, jyy, jzz = jx * ux, jy * uy, jz * uz
        ju = jxx + jyy + jzz
        ne = (1.19 * 19.0 / 2394.0) * (diag - f[0] - ju)
        neps = (1.4 / 252.0) * (9.0 * f[0] - 7.0 * axis - 2.0 * diag + 5.5 * ju)
        ax_part = -11.0 * ne - 4.0 * neps
        dg_part = 8.0 * ne + neps
        eq_xx = 3.0 * jxx - ju
        eq_ww = jyy - jzz
        axis_xx, diag_xx = 3.0 * sx - axis, diag - 3.0 * yz
        axis_ww, diag_ww = sy - sz, xy - xz
        pi_xx = (1.4 / 72.0) * (diag_xx - 2.0 * axis_xx + 0.5 * eq_xx)
        pi_ww = (1.4 / 24.0) * (diag_ww - 2.0 * axis_ww + 0.5 * eq_ww)
        shear[XX, i + 1, inner, :] = (1.0 / 36.0) * (axis_xx + diag_xx - eq_xx)
        shear[WW, i + 1, inner, :] = (1.0 / 12.0) * (axis_ww + diag_ww - eq_ww)
        shear[XY, i + 1, inner, :] = 0.25 * (sa - sb - jx * uy)
        shear[XZ, i + 1, inner, :] = 0.25 * (sc - sd - jx * uz)
        shear[YZ, i + 1, inner, :] = 0.25 * (se - sg - jy * uz)
        two_xx, two_ww = 2.0 * pi_xx, 2.0 * pi_ww
        base_yz = ax_part + two_xx
        hx = ax_part - 2.0 * two_xx
        hy, hz = base_yz - two_ww, base_yz + two_ww
        base_d = dg_part + pi_xx
        hxy, hxz, hyz = base_d + pi_ww, base_d - pi_ww, dg_part - two_xx
        tx = (1.2 / 8.0) * ((1.0 / 3.0) * jx - dx)
        ty = (1.2 / 8.0) * ((1.0 / 3.0) * jy - dy)
        tz = (1.2 / 8.0) * ((1.0 / 3.0) * jz - dz)
        mx = (1.98 / 8.0) * (abp - cdp)
        my = (1.98 / 8.0) * (egp - abm)
        mz = (1.98 / 8.0) * (cdm - egm)
        xp, xm, yp, ym, zp, zm = tx + mx, tx - mx, ty + my, ty - my, tz + mz, tz - mz
        halves = [
            (hx, -4.0 * tx),
            (hy, -4.0 * ty),
            (hz, -4.0 * tz),
            (hxy, xp + ym),
            (hxy, xp - ym),
            (hxz, xm + zp),
            (hxz, xm - zp),
            (hyz, yp + zm),
            (hyz, yp - zm),
        ]
        post[PLACE[0], i + 1, inner, :] = f[0] + (30.0 * ne - 12.0 * neps)
        for n, (even, odd) in enumerate(halves):
            post[PLACE[2 * n + 1], i + 1, inner, :] = f[2 * n + 1] - (even + odd)
            post[PLACE[2 * n + 2], i + 1, inner, :] = f[2 * n + 2] - (even - odd)
        return carry

    lax.fori_loop(0, cz, collide_plane, 0)

    crossing = [
        ((1, 0), 0, 5),
        ((-1, 0), 8, 5),
        ((0, 1), 4, 5),
        ((0, -1), 12, 4),
        ((0, -1), 0, 1),
        ((1, 1), 4, 1),
        ((1, -1), 0, 1),
        ((-1, 1), 8, 1),
        ((-1, -1), 12, 1),
    ]

    def halo_copy(ref, side, first_of, count, send, recv):
        dz, dy = side
        zs, zt = ranges(dz, 1, cz, 1)
        ys, yt = ranges(dy, ROW, cy, 1)
        group = pl.ds(first_of, count)
        return pltpu.make_async_remote_copy(
            src_ref=ref.at[group, zs, ys, :],
            dst_ref=ref.at[group, zt, yt, :],
            send_sem=send,
            recv_sem=recv,
            device_id=near(split, dz, dy),
            device_id_type=MESH,
        )

    halo = []
    for i, (side, first_of, count) in enumerate(crossing):
        halo.append(halo_copy(post, side, first_of, count, p_send.at[i], p_recv.at[i]))
    for i, side in enumerate(SIDES):
        first_of = 0 if side[1] == 0 else (1 if side[0] == 0 else 1)
        count = 3 if side[0] and side[1] else 4
        halo.append(halo_copy(shear, side, first_of, count, s_send.at[i], s_recv.at[i]))

    for copy in halo:
        copy.start()

    d1r[xc] = d1s[xc]
    for_others(xc, nxc, lambda j: d1_copy(j, j).wait_recv())
    total = d1r[0]
    for j in range(1, nxc):
        total = total + d1r[j]
    d2[z] = total
    for_others(z, nz, lambda j: d2_copy(j, z).start())

    kk, nmark = cell_ref.shape
    nrows = cz * cy
    row_iota = lax.broadcasted_iota(jnp.int32, (nmark, nrows), 1)
    lane_iota = lax.broadcasted_iota(jnp.int32, (nmark, cx), 1)
    cells = jnp.transpose(cell_ref[...], (1, 0))
    weights = jnp.transpose(weight_ref[...], (1, 0))
    for k in range(kk):
        cell = cells[:, k : k + 1]
        line = cell // cx
        block = pl.ds(k * nmark, nmark)
        picked = jnp.where(row_iota == line, 1.0, 0.0).astype(jnp.bfloat16)
        pick[block, 0:nrows] = picked
        pick[block, nrows : 2 * nrows] = picked
        lanes[block, :] = jnp.where(lane_iota == cell - line * cx, weights[:, k : k + 1], 0.0)
    ids = seg_ref[...].reshape(1, nmark)
    lane_count = SEG_DEV * ng2
    seg_iota = lax.broadcasted_iota(jnp.int32, (lane_count, nmark), 0)
    for j in range(ng1):
        hot[j] = jnp.where(seg_iota == ids - j * lane_count, 1.0, 0.0).astype(jnp.bfloat16)

    for_others(z, nz, lambda j: d2_copy(j, j).wait_recv())
    total = d2[0]
    for j in range(1, nz):
        total = total + d2[j]
    d1s[xc] = total
    eddy_rows = jnp.maximum(d1s[xc, 0:rows, :] / (d1s[xc, rows : 2 * rows, :] + eps_sum), 0.0)
    d3[xc, 0:rows, :] = eddy_rows
    d3[xc, rows : 2 * rows, :] = eddy_rows
    for_others(xc, nxc, lambda j: d3_copy(j, xc).start())

    @pl.when(last)
    def _():
        for_all(nxc, lambda j: edge_copy(j, 0).start())

    @pl.when(first)
    def _():
        for_all(nxc, lambda j: edge_copy(j, 1).start())

    for copy in halo:
        copy.wait()
    for_others(xc, nxc, lambda j: d3_copy(j, j).wait_recv())
    for side in range(2):
        edge_copy(0, side).wait_recv()
    for j in range(nxc):
        eddy_ref[j * rows : (j + 1) * rows, :] = d3[j, 0:rows, :]
        eddyx[ROW + j * rows : ROW + (j + 1) * rows, :] = d3[j, 0:rows, :]
    eddyx[ROW - 1 : ROW, :] = dlow[rows - 1 : rows, :]
    eddyx[ROW + cy : ROW + cy + 1, :] = dhigh[0:1, :]

    def relax(p, start, count, which):
        here = pl.ds(start, count)
        mag = mags[p, pl.ds(start - ROW + 1, count), :]
        rate = 1.0 / (0.5 + 3.0 * (base_visc + eddyx[here, :] * mag))
        parts = {}

        def moment(n):
            if n not in parts:
                parts[n] = rate * shear[n, p, here, :]
            return parts[n]

        def lost(n):
            if n in parts:
                return parts[n]
            if n == "y":
                value = moment(XX) + moment(WW)
            elif n == "z":
                value = moment(XX) - moment(WW)
            else:
                value = -2.0 * moment(XX)
            parts[n] = value
            return value

        rules = [
            lambda: 2.0 * moment(XX),
            lambda: moment(WW) - moment(XX),
            lambda: -lost("y"),
            lambda: lost("y") + moment(XY),
            lambda: lost("y") - moment(XY),
            lambda: lost("z") + moment(XZ),
            lambda: lost("z") - moment(XZ),
            lambda: lost("yz") + moment(YZ),
            lambda: lost("yz") - moment(YZ),
        ]
        for q in which:
            value = post[PLACE[q], p, here, :]
            if q:
                pair = (q - 1) // 2
                if ("pair", pair) not in parts:
                    parts["pair", pair] = rules[pair]()
                value = value - parts["pair", pair]
            post[PLACE[q], p, here, :] = value.astype(jnp.bfloat16).astype(jnp.float32)

    def going(dz, dy):
        return [
            q
            for q, (ex, ey, ez) in enumerate(VELOCITIES)
            if (dz == 0 or ez == dz) and (dy == 0 or ey == dy)
        ]

    def finish_plane(i, carry):
        relax(i, ROW, cy, range(19))
        relax(i, ROW - 1, 1, going(0, 1))
        relax(i, ROW + cy, 1, going(0, -1))
        return carry

    lax.fori_loop(1, cz + 1, finish_plane, 0)
    for p, dz in ((0, 1), (cz + 1, -1)):
        relax(p, ROW, cy, going(dz, 0))
        relax(p, ROW - 1, 1, going(dz, 1))
        relax(p, ROW + cy, 1, going(dz, -1))

    def stream_plane(i, carry):
        f = []
        for q, (ex, ey, ez) in enumerate(VELOCITIES):
            value = post[PLACE[q], i + 1 - ez, pl.ds(ROW - ey, cy), :]
            if ex:
                value = roll_x(value, ex)
            outv[q, i] = value.astype(jnp.bfloat16)
            f.append(value)
        d = [f[2 * n + 1] - f[2 * n + 2] for n in range(9)]
        jx = d[0] + (d[3] + d[4]) + (d[5] + d[6])
        jy = d[1] + (d[3] - d[4]) + (d[7] + d[8])
        jz = d[2] + (d[5] - d[6]) + (d[7] - d[8])
        lines = pl.ds(pl.multiple_of(i * cy, cy), cy)
        lower = pl.ds(pl.multiple_of(nrows + i * cy, cy), cy)
        for n, value in enumerate((jx, jy, jz)):
            high = value.astype(jnp.bfloat16)
            low = (value - high.astype(jnp.float32)).astype(jnp.bfloat16)
            mom[lines, n * cx : (n + 1) * cx] = high
            mom[lower, n * cx : (n + 1) * cx] = low
        return carry

    lax.fori_loop(0, cz, stream_plane, 0)

    gath[...] = jnp.dot(pick[...], mom[...], preferred_element_type=jnp.float32)

    def parts_of(value):
        first_part = value.astype(jnp.bfloat16)
        return first_part, (value - first_part.astype(jnp.float32)).astype(jnp.bfloat16)

    def dot_t(a, b):
        return lax.dot_general(a, b, (((1,), (1,)), ((), ())), preferred_element_type=jnp.float32)

    ones = jnp.ones((16, cx), jnp.bfloat16)
    forces = []
    for n in range(3):
        acc = None
        for k in range(kk):
            block = pl.ds(k * nmark, nmark)
            term = lanes[block, :] * gath[block, n * cx : (n + 1) * cx]
            acc = term if acc is None else acc + term
        a, b = parts_of(acc)
        forces.append(-(dot_t(ones, a) + dot_t(ones, b))[0:8])
    which = lax.broadcasted_iota(jnp.int32, (8, nmark), 0)
    force = jnp.where(which == 0, forces[0], jnp.where(which == 1, forces[1], forces[2]))
    a, b = parts_of(force)
    both = jnp.concatenate([a.astype(jnp.float32), b.astype(jnp.float32)], axis=0).astype(jnp.bfloat16)
    for j in range(ng1):
        sums_of = dot_t(both, hot[j])
        h1s[j] = sums_of[0:8] + sums_of[8:16]

    for_others(g1, ng1, lambda j: h1_copy(j, g1).start())
    h1r[g1] = h1s[g1]
    for_others(g1, ng1, lambda j: h1_copy(j, j).wait_recv())
    total = h1r[0]
    for j in range(1, ng1):
        total = total + h1r[j]
    h2[g2] = total
    for_others(g2, ng2, lambda j: h2_copy(j, g2).start())

    for_others(xc, nxc, lambda j: d1_copy(j, xc).wait_send())
    for_others(z, nz, lambda j: d2_copy(j, z).wait_send())
    for_others(xc, nxc, lambda j: d3_copy(j, xc).wait_send())
    for_others(g1, ng1, lambda j: h1_copy(j, g1).wait_send())

    @pl.when(last)
    def _():
        for_all(nxc, lambda j: edge_copy(j, 0).wait_send())

    @pl.when(first)
    def _():
        for_all(nxc, lambda j: edge_copy(j, 1).wait_send())

    for_others(g2, ng2, lambda j: h2_copy(j, j).wait_recv())
    total = h2[0]
    for j in range(1, ng2):
        total = total + h2[j]
    mine = pltpu.roll(total, (lane_count - place * SEG_DEV) % lane_count, axis=1)
    force_ref[...] = mine[0:3, 0:SEG_DEV]
    for_others(g2, ng2, lambda j: h2_copy(j, g2).wait_send())


def write_kernel(outv, eddy, force, out_hbm, eddy_hbm, force_hbm, sem):
    copies = [
        pltpu.make_async_copy(outv, out_hbm, sem.at[0]),
        pltpu.make_async_copy(eddy, eddy_hbm, sem.at[1]),
        pltpu.make_async_copy(force, force_hbm, sem.at[2]),
    ]
    for copy in copies:
        copy.start()
    for copy in copies:
        copy.wait()


def local(split, populations, cell_index, marker_weight, segment_id):
    nq, cz, cy, cx = populations.shape
    nmark, kk = cell_index.shape
    nz, nx, nc, ny = split
    nxc = nx * nc
    ng1, ng2 = nz * (nx // 2), 2 * nc * ny
    rows = cy // nxc
    f32, bf16 = jnp.float32, jnp.bfloat16
    dma = pltpu.SemaphoreType.DMA
    vmem = pl.BlockSpec(memory_space=pltpu.VMEM)
    hbm = pl.BlockSpec(memory_space=pltpu.HBM)
    lane_count = SEG_DEV * ng2
    velocity = pl.pallas_call(
        functools.partial(velocity_kernel, split),
        out_shape=pltpu.VMEM((3, cz + 4, TOP, cx), f32),
        in_specs=[hbm],
        out_specs=vmem,
        scratch_shapes=[
            pltpu.VMEM((nq, cz, cy, cx), bf16),
            dma((4,)),
            dma((8,)),
            dma((8,)),
        ],
        compiler_params=pltpu.CompilerParams(
            collective_id=0, has_side_effects=True, vmem_limit_bytes=8 * 1024 * 1024
        ),
    )(pltpu.with_memory_space_constraint(populations, pltpu.HBM))
    scratch = [
        pltpu.VMEM((3 * cx, cx), bf16),
        pltpu.VMEM((12, cy, cx), f32),
        pltpu.VMEM((12, cy, cx), f32),
        pltpu.VMEM((cz + 2, 40, cx), f32),
        pltpu.VMEM((12, 40, cx), f32),
        pltpu.VMEM((12, 40, cx), f32),
        pltpu.VMEM((3, 48, cx), f32),
        pltpu.VMEM((3, 48, cx), f32),
        pltpu.VMEM((3, cz + 3, 40, cx), f32),
        pltpu.VMEM((12, cz + 4, cy, cx), f32),
        pltpu.VMEM((2, cy, cx), f32),
        pltpu.VMEM((5, cz + 2, TOP, cx), f32),
        pltpu.VMEM((nq, cz + 2, TOP, cx), f32),
        pltpu.VMEM((TOP, cx), f32),
        pltpu.VMEM((2 * cz * cy, 3 * cx), bf16),
        pltpu.VMEM((kk * nmark, 2 * cz * cy), bf16),
        pltpu.VMEM((kk * nmark, cx), f32),
        pltpu.VMEM((kk * nmark, 3 * cx), f32),
        pltpu.VMEM((ng1, lane_count, nmark), bf16),
        pltpu.VMEM((nxc, 2 * rows, cx), f32),
        pltpu.VMEM((nxc, 2 * rows, cx), f32),
        pltpu.VMEM((nz, 2 * rows, cx), f32),
        pltpu.VMEM((nxc, 2 * rows, cx), f32),
        pltpu.VMEM((2 * rows, cx), f32),
        pltpu.VMEM((2 * rows, cx), f32),
        pltpu.VMEM((ng1, 8, lane_count), f32),
        pltpu.VMEM((ng1, 8, lane_count), f32),
        pltpu.VMEM((ng2, 8, lane_count), f32),
        dma((9,)),
        dma((9,)),
        dma((8,)),
        dma((8,)),
        dma((nxc,)),
        dma((nxc,)),
        dma((nz,)),
        dma((nz,)),
        dma((nxc,)),
        dma((nxc,)),
        dma((2, nxc)),
        dma((2,)),
        dma((ng1,)),
        dma((ng1,)),
        dma((ng2,)),
        dma((ng2,)),
    ]
    results = pl.pallas_call(
        functools.partial(step_kernel, split),
        out_shape=(
            pltpu.VMEM((nq, cz, cy, cx), bf16),
            pltpu.VMEM((cy, cx), f32),
            pltpu.VMEM((3, SEG_DEV), f32),
        ),
        in_specs=[vmem, vmem, vmem, vmem, vmem],
        out_specs=(vmem, vmem, vmem),
        scratch_shapes=scratch,
        compiler_params=pltpu.CompilerParams(
            collective_id=1, has_side_effects=True, vmem_limit_bytes=40 * 1024 * 1024
        ),
    )(velocity, populations, cell_index.T, marker_weight.T, segment_id)
    return pl.pallas_call(
        write_kernel,
        out_shape=(
            jax.ShapeDtypeStruct((nq, cz, cy, cx), bf16),
            jax.ShapeDtypeStruct((cy, cx), f32),
            jax.ShapeDtypeStruct((3, SEG_DEV), f32),
        ),
        in_specs=[vmem, vmem, vmem],
        out_specs=(hbm, hbm, hbm),
        scratch_shapes=[dma((3,))],
        compiler_params=pltpu.CompilerParams(vmem_limit_bytes=1024 * 1024),
    )(*results)


def solution(mesh):
    in_specs = (
        P(None, "span", "cross", None),
        P(("span", "cross"), None),
        P(("span", "cross"), None),
        P(("span", "cross")),
    )
    out_specs = (P(None, "span", "cross", None), P("cross", None), P(None, ("span", "cross")))
    sizes = dict(mesh.shape)
    split = (sizes["span"] // (CHIPS_X * CORES), CHIPS_X, CORES, sizes["cross"])
    return jax.shard_map(
        functools.partial(local, split),
        mesh=mesh,
        in_specs=in_specs,
        out_specs=out_specs,
        check_vma=False,
    )
```

```python
import functools

import jax
import jax.numpy as jnp
from jax import lax
from jax.experimental import pallas as pl
from jax.experimental.pallas import tpu as pltpu
from jax.sharding import PartitionSpec as P

SEG_DEV = 8
MESH = pl.DeviceIdType.MESH
eps_sum = 1e-06
base_visc = 0.005

CHIPS_X = 4
CORES = 2

VELOCITIES = [
    (0, 0, 0),
    (1, 0, 0),
    (-1, 0, 0),
    (0, 1, 0),
    (0, -1, 0),
    (0, 0, 1),
    (0, 0, -1),
    (1, 1, 0),
    (-1, -1, 0),
    (1, -1, 0),
    (-1, 1, 0),
    (1, 0, 1),
    (-1, 0, -1),
    (1, 0, -1),
    (-1, 0, 1),
    (0, 1, 1),
    (0, -1, -1),
    (0, 1, -1),
    (0, -1, 1),
]
ORDER = [18, 5, 11, 14, 15, 3, 7, 10, 17, 6, 12, 13, 16, 4, 8, 9, 0, 1, 2]
PLACE = [ORDER.index(q) for q in range(19)]

ROW = 8
TOP = 48


def add_pairs(f):
    s = [f[2 * i + 1] + f[2 * i + 2] for i in range(9)]
    d = [f[2 * i + 1] - f[2 * i + 2] for i in range(9)]
    return s, d


def tri(low, mid, high):
    return (low + high) + (mid + mid)


def roll_x(a, shift):
    return pltpu.roll(a, shift % a.shape[-1], axis=a.ndim - 1)


def strain_of(d):
    exy, exz, eyz = d[0][1] + d[1][0], d[0][2] + d[2][0], d[1][2] + d[2][1]
    diag = d[0][0] * d[0][0] + d[1][1] * d[1][1] + d[2][2] * d[2][2]
    off = exy * exy + exz * exz + eyz * eyz
    mag = jnp.sqrt(0.5 * diag + 0.25 * off)
    return (d[0][0], d[1][1], d[2][2], exy, exz, eyz), mag


PAIRS = [(0, 0), (1, 1), (2, 2), (0, 1), (0, 2), (1, 2)]


SIDES = [(1, 0), (-1, 0), (0, 1), (0, -1), (1, 1), (1, -1), (-1, 1), (-1, -1)]
XZ, XX, WW, YZ, XY = range(5)


def near(split, dz, dy):
    nz, nx, nc, ny = split
    nspan = nz * nx * nc
    s, y = lax.axis_index("span"), lax.axis_index("cross")
    return ((s + dz + nspan) % nspan, (y + dy + ny) % ny)


def ranges(d, first, size, width):
    if d == 0:
        return pl.ds(first, size), pl.ds(first, size)
    if d > 0:
        return pl.ds(first + size - width, width), pl.ds(first - width, width)
    return pl.ds(first, width), pl.ds(first + size, width)


def velocity_kernel(split, pops_hbm, vel, pops, in_sem, v_send, v_recv):
    cz, cy, cx = pops.shape[1:]
    nchunk = in_sem.shape[0]
    step = cz // nchunk

    def fetch(i):
        some = pl.ds(i * step, step)
        return pltpu.make_async_copy(pops_hbm.at[:, some], pops.at[:, some], in_sem.at[i])

    order = [0, nchunk - 1] + list(range(1, nchunk - 1))
    for i in order:
        fetch(i).start()
    barrier = pltpu.get_barrier_semaphore()
    for dz, dy in SIDES:
        pl.semaphore_signal(
            barrier, inc=1, device_id=near(split, dz, dy), device_id_type=MESH
        )

    def moments_plane(i, carry):
        f = [pops[q, i].astype(jnp.float32) for q in range(19)]
        sm, d = add_pairs(f)
        density = f[0] + ((sm[0] + sm[1] + sm[2]) + (sm[3] + sm[4] + sm[5]) + (sm[6] + sm[7] + sm[8]))
        jx = d[0] + (d[3] + d[4]) + (d[5] + d[6])
        jy = d[1] + (d[3] - d[4]) + (d[7] + d[8])
        jz = d[2] + (d[5] - d[6]) + (d[7] - d[8])
        inv = 1.0 / density
        inner = pl.ds(ROW, cy)
        vel[0, i + 2, inner, :] = jx * inv
        vel[1, i + 2, inner, :] = jy * inv
        vel[2, i + 2, inner, :] = jz * inv
        return carry

    def moments_of(i):
        fetch(i).wait()
        lax.fori_loop(i * step, (i + 1) * step, moments_plane, 0)

    def vel_copy(i):
        dz, dy = SIDES[i]
        zs, zt = ranges(dz, 2, cz, 2)
        ys, yt = ranges(dy, ROW, cy, 2)
        return pltpu.make_async_remote_copy(
            src_ref=vel.at[:, zs, ys, :],
            dst_ref=vel.at[:, zt, yt, :],
            send_sem=v_send.at[i],
            recv_sem=v_recv.at[i],
            device_id=near(split, dz, dy),
            device_id_type=MESH,
        )

    for i in order[:2]:
        moments_of(i)
    pl.semaphore_wait(barrier, len(SIDES))
    for i, (dz, dy) in enumerate(SIDES):
        if dz:
            vel_copy(i).start()
    for i in order[2:]:
        moments_of(i)
    for i, (dz, dy) in enumerate(SIDES):
        if not dz:
            vel_copy(i).start()
    for i in range(len(SIDES)):
        vel_copy(i).wait()


def step_kernel(
    split,
    vel,
    pops,
    cell_ref,
    weight_ref,
    seg_ref,
    outv,
    eddy_ref,
    force_ref,
    smoother,
    hats_a,
    hats_b,
    mags,
    tmp_a,
    tmp_b,
    vtmp_a,
    vtmp_b,
    vhat,
    filt,
    sums,
    shear,
    post,
    eddyx,
    mom,
    pick,
    lanes,
    gath,
    hot,
    d1s,
    d1r,
    d2,
    d3,
    dlow,
    dhigh,
    h1s,
    h1r,
    h2,
    p_send,
    p_recv,
    s_send,
    s_recv,
    d1_send,
    d1_recv,
    d2_send,
    d2_recv,
    d3_send,
    d3_recv,
    e_send,
    e_recv,
    h1_send,
    h1_recv,
    h2_send,
    h2_recv,
):
    nz, nx, nc, ny = split
    nxc = nx * nc
    cz, cy, cx = pops.shape[1:]
    half = nx // 2
    ng1, ng2 = nz * half, 2 * nc * ny
    s = lax.axis_index("span")
    y = lax.axis_index("cross")
    z, xc = s // nxc, s % nxc
    x, c = xc // nc, xc % nc
    g1 = z * half + x // 2
    g2 = y * (2 * nc) + (x % 2) * nc + c
    place = (x % 2) * (nc * ny) + c * ny + y
    y_up, y_down = (y + 1) % ny, (y + ny - 1) % ny

    def xc_dev(k):
        return (s - xc + (xc + k) % nxc, y)

    def z_dev(k):
        return ((s + nxc * k) % (nz * nxc), y)

    def g1_dev(k):
        return ((s + 2 * nc * k) % (nz * nxc), y)

    def g2_dev(k):
        other = (g2 + k) % ng2
        return (s - s % (2 * nc) + other % (2 * nc), other // (2 * nc))

    def for_others(me, count, act):
        for k in sorted(range(1, count), key=lambda k: abs(2 * k - count)):
            act(k, (me + k) % count)

    def for_all(count, act):
        def body(j, carry):
            act(j)
            return carry

        lax.fori_loop(0, count, body, 0)

    barrier = pltpu.get_barrier_semaphore()

    def greet(dev):
        pl.semaphore_signal(barrier, inc=1, device_id=dev, device_id_type=MESH)

    for_others(g1, ng1, lambda k, j: greet(g1_dev(k)))
    for_others(g2, ng2, lambda k, j: greet(g2_dev(k)))
    for_others(z, nz, lambda k, j: greet(z_dev(k)))
    for_others(xc, nxc, lambda k, j: greet(xc_dev(k)))
    for dz, dy in SIDES:
        greet(near(split, dz, dy))
    greet((z * nxc + nxc - 1, y_down))
    greet((z * nxc, y_up))
    last, first = xc == nxc - 1, xc == 0
    greeted = len(SIDES) + (nxc - 1) + (nz - 1) + (ng1 - 1) + (ng2 - 1)
    greeted = greeted + jnp.where(jnp.logical_or(last, first), nxc, 0)

    apart = lax.broadcasted_iota(jnp.int32, (cx, cx), 0) - lax.broadcasted_iota(jnp.int32, (cx, cx), 1)
    apart = (apart + cx) % cx
    beside = jnp.logical_or(apart == 1, apart == cx - 1)
    circulant = jnp.where(apart == 0, 2.0, jnp.where(beside, 1.0, 0.0)).astype(jnp.bfloat16)
    for n in range(3):
        smoother[n * cx : (n + 1) * cx, :] = circulant

    def smooth_x(values):
        both = jnp.concatenate(values, axis=0)
        high = both.astype(jnp.bfloat16)
        rest = both - high.astype(jnp.float32)
        mid = rest.astype(jnp.bfloat16)
        low = (rest - mid.astype(jnp.float32)).astype(jnp.bfloat16)
        parts = jnp.concatenate([high, mid, low], axis=1)
        return jnp.dot(parts, smoother[...], preferred_element_type=jnp.float32)

    def products(p, tmp, vtmp):
        mid, low, high = pl.ds(ROW - 1, 40), pl.ds(ROW - 2, 40), pl.ds(ROW, 40)
        v = [vel[a, p + 1, mid, :] for a in range(3)]
        for n, (a, b) in enumerate(PAIRS):
            tmp[n + 6] = v[a] * v[b]
        d = []
        for a in range(3):
            below = vel[a, p + 1, low, :]
            vtmp[a, 0:40, :] = tri(vel[a, p, low, :], below, vel[a, p + 2, low, :])
            dx = roll_x(v[a], -1) - roll_x(v[a], 1)
            dy = vel[a, p + 1, high, :] - below
            dz = vel[a, p + 2, mid, :] - vel[a, p, mid, :]
            d.append((dx, dy, dz))
        e, mag = strain_of(d)
        mags[p] = mag
        half_mag = 0.5 * mag
        for n in range(3):
            tmp[n] = mag * e[n]
            tmp[n + 3] = half_mag * e[n + 3]

    def filters(p, tmp, vtmp):
        for n in range(12):
            filt[n, p + 1] = tri(tmp[n, 0:cy, :], tmp[n, 1 : cy + 1, :], tmp[n, 2 : cy + 2, :])
        along_y = [tri(vtmp[a, 0:40, :], vtmp[a, 1:41, :], vtmp[a, 2:42, :]) for a in range(3)]
        smoothed = smooth_x(along_y)
        for a in range(3):
            vhat[a, p + 1] = (1.0 / 64.0) * smoothed[a * 40 : (a + 1) * 40]

    def two_planes(i, carry):
        products(2 * i, tmp_a, vtmp_a)
        filters(2 * i - 1, tmp_b, vtmp_b)
        products(2 * i + 1, tmp_b, vtmp_b)
        filters(2 * i, tmp_a, vtmp_a)
        return carry

    lax.fori_loop(0, (cz + 2) // 2, two_planes, 0)
    filters(cz + 1, tmp_b, vtmp_b)

    def hats_of(i, hats):
        along_z = [tri(filt[n, i + 1], filt[n, i + 2], filt[n, i + 3]) for n in range(12)]
        smoothed = smooth_x(along_z)
        for n in range(12):
            hats[n] = (1.0 / 64.0) * smoothed[n * cy : (n + 1) * cy]

    def add_plane(i, hats, plane_lm, plane_mm):
        mid, low, high = pl.ds(1, cy), pl.ds(0, cy), pl.ds(2, cy)
        v = [vhat[a, i + 2, mid, :] for a in range(3)]
        d = []
        for a in range(3):
            dx = roll_x(v[a], -1) - roll_x(v[a], 1)
            dy = vhat[a, i + 2, high, :] - vhat[a, i + 2, low, :]
            dz = vhat[a, i + 3, mid, :] - vhat[a, i + 1, mid, :]
            d.append((dx, dy, dz))
        e, mag = strain_of(d)
        four, two = 4.0 * mag, 2.0 * mag
        lm = mm = lm_off = mm_off = None
        for n, (a, b) in enumerate(PAIRS):
            model = hats[n] - (four if n < 3 else two) * e[n]
            leonard = hats[n + 6] - v[a] * v[b]
            if n == 0:
                lm, mm = leonard * model, model * model
            elif n < 3:
                lm, mm = lm + leonard * model, mm + model * model
            elif n == 3:
                lm_off, mm_off = leonard * model, model * model
            else:
                lm_off, mm_off = lm_off + leonard * model, mm_off + model * model
        return plane_lm + (lm + 2.0 * lm_off), plane_mm + (mm + 2.0 * mm_off)

    def second_pass(i, carry):
        hats_of(2 * i + 1, hats_b)
        carry = add_plane(2 * i, hats_a, *carry)
        hats_of(2 * i + 2, hats_a)
        return add_plane(2 * i + 1, hats_b, *carry)

    zero = jnp.zeros((cy, cx), jnp.float32)
    hats_of(0, hats_a)
    plane_lm, plane_mm = lax.fori_loop(0, cz // 2, second_pass, (zero, zero))

    rows = cy // nxc
    sums[0] = plane_lm
    sums[1] = plane_mm
    for j in range(nxc):
        d1s[j, 0:rows, :] = sums[0, j * rows : (j + 1) * rows, :]
        d1s[j, rows : 2 * rows, :] = sums[1, j * rows : (j + 1) * rows, :]

    def exchange(src, dst, slot, send, recv, dev, k):
        return pltpu.make_async_remote_copy(
            src_ref=src,
            dst_ref=dst.at[slot],
            send_sem=send.at[k],
            recv_sem=recv.at[slot],
            device_id=dev(k),
            device_id_type=MESH,
        )

    def d1_copy(k, j, slot):
        return exchange(d1s.at[j], d1r, slot, d1_send, d1_recv, xc_dev, k)

    def d2_copy(k, j, slot):
        return exchange(d2.at[z], d2, slot, d2_send, d2_recv, z_dev, k)

    def d3_copy(k, j, slot):
        return exchange(d3.at[xc], d3, slot, d3_send, d3_recv, xc_dev, k)

    def edge_copy(j, side):
        return pltpu.make_async_remote_copy(
            src_ref=d3.at[xc],
            dst_ref=dlow if side == 0 else dhigh,
            send_sem=e_send.at[side, j],
            recv_sem=e_recv.at[side],
            device_id=(z * nxc + j, y_up if side == 0 else y_down),
            device_id_type=MESH,
        )

    def h1_copy(k, j, slot):
        return exchange(h1s.at[j], h1r, slot, h1_send, h1_recv, g1_dev, k)

    def h2_copy(k, j, slot):
        return exchange(h2.at[g2], h2, slot, h2_send, h2_recv, g2_dev, k)

    pl.semaphore_wait(barrier, greeted)
    for_others(xc, nxc, lambda k, j: d1_copy(k, j, xc).start())

    inner = pl.ds(ROW, cy)

    def collide_plane(i, carry):
        f = [pops[q, i].astype(jnp.float32) for q in range(19)]
        sm, d = add_pairs(f)
        sx, sy, sz, sa, sb, sc, sd, se, sg = sm
        dx, dy, dz, da, db, dc, dd, de, dg = d
        ux, uy, uz = [vel[a, i + 2, inner, :] for a in range(3)]
        xy, xz, yz = sa + sb, sc + sd, se + sg
        axis, diag = sx + sy + sz, xy + xz + yz
        abp, abm, cdp, cdm, egp, egm = da + db, da - db, dc + dd, dc - dd, de + dg, de - dg
        jx, jy, jz = dx + (abp + cdp), dy + (abm + egp), dz + (cdm + egm)
        jxx, jyy, jzz = jx * ux, jy * uy, jz * uz
        ju = jxx + jyy + jzz
        ne = (1.19 * 19.0 / 2394.0) * (diag - f[0] - ju)
        neps = (1.4 / 252.0) * (9.0 * f[0] - 7.0 * axis - 2.0 * diag + 5.5 * ju)
        ax_part = -11.0 * ne - 4.0 * neps
        dg_part = 8.0 * ne + neps
        eq_xx = 3.0 * jxx - ju
        eq_ww = jyy - jzz
        axis_xx, diag_xx = 3.0 * sx - axis, diag - 3.0 * yz
        axis_ww, diag_ww = sy - sz, xy - xz
        pi_xx = (1.4 / 72.0) * (diag_xx - 2.0 * axis_xx + 0.5 * eq_xx)
        pi_ww = (1.4 / 24.0) * (diag_ww - 2.0 * axis_ww + 0.5 * eq_ww)
        shear[XX, i + 1, inner, :] = (1.0 / 36.0) * (axis_xx + diag_xx - eq_xx)
        shear[WW, i + 1, inner, :] = (1.0 / 12.0) * (axis_ww + diag_ww - eq_ww)
        shear[XY, i + 1, inner, :] = 0.25 * (sa - sb - jx * uy)
        shear[XZ, i + 1, inner, :] = 0.25 * (sc - sd - jx * uz)
        shear[YZ, i + 1, inner, :] = 0.25 * (se - sg - jy * uz)
        two_xx, two_ww = 2.0 * pi_xx, 2.0 * pi_ww
        base_yz = ax_part + two_xx
        hx = ax_part - 2.0 * two_xx
        hy, hz = base_yz - two_ww, base_yz + two_ww
        base_d = dg_part + pi_xx
        hxy, hxz, hyz = base_d + pi_ww, base_d - pi_ww, dg_part - two_xx
        tx = (1.2 / 8.0) * ((1.0 / 3.0) * jx - dx)
        ty = (1.2 / 8.0) * ((1.0 / 3.0) * jy - dy)
        tz = (1.2 / 8.0) * ((1.0 / 3.0) * jz - dz)
        mx = (1.98 / 8.0) * (abp - cdp)
        my = (1.98 / 8.0) * (egp - abm)
        mz = (1.98 / 8.0) * (cdm - egm)
        xp, xm, yp, ym, zp, zm = tx + mx, tx - mx, ty + my, ty - my, tz + mz, tz - mz
        halves = [
            (hx, -4.0 * tx),
            (hy, -4.0 * ty),
            (hz, -4.0 * tz),
            (hxy, xp + ym),
            (hxy, xp - ym),
            (hxz, xm + zp),
            (hxz, xm - zp),
            (hyz, yp + zm),
            (hyz, yp - zm),
        ]
        post[PLACE[0], i + 1, inner, :] = f[0] + (30.0 * ne - 12.0 * neps)
        for n, (even, odd) in enumerate(halves):
            post[PLACE[2 * n + 1], i + 1, inner, :] = f[2 * n + 1] - (even + odd)
            post[PLACE[2 * n + 2], i + 1, inner, :] = f[2 * n + 2] - (even - odd)
        return carry

    lax.fori_loop(0, cz, collide_plane, 0)

    crossing = [
        ((1, 0), 0, 5),
        ((-1, 0), 8, 5),
        ((0, 1), 4, 5),
        ((0, -1), 12, 4),
        ((0, -1), 0, 1),
        ((1, 1), 4, 1),
        ((1, -1), 0, 1),
        ((-1, 1), 8, 1),
        ((-1, -1), 12, 1),
    ]

    def halo_copy(ref, side, first_of, count, send, recv):
        dz, dy = side
        zs, zt = ranges(dz, 1, cz, 1)
        ys, yt = ranges(dy, ROW, cy, 1)
        group = pl.ds(first_of, count)
        return pltpu.make_async_remote_copy(
            src_ref=ref.at[group, zs, ys, :],
            dst_ref=ref.at[group, zt, yt, :],
            send_sem=send,
            recv_sem=recv,
            device_id=near(split, dz, dy),
            device_id_type=MESH,
        )

    halo = []
    for i, (side, first_of, count) in enumerate(crossing):
        halo.append(halo_copy(post, side, first_of, count, p_send.at[i], p_recv.at[i]))
    for i, side in enumerate(SIDES):
        first_of = 0 if side[1] == 0 else (1 if side[0] == 0 else 1)
        count = 3 if side[0] and side[1] else 4
        halo.append(halo_copy(shear, side, first_of, count, s_send.at[i], s_recv.at[i]))

    for copy in halo:
        copy.start()

    d1r[xc] = d1s[xc]
    for_others(xc, nxc, lambda k, j: d1_copy(k, j, j).wait_recv())
    total = d1r[0]
    for j in range(1, nxc):
        total = total + d1r[j]
    d2[z] = total
    for_others(z, nz, lambda k, j: d2_copy(k, j, z).start())

    kk, nmark = cell_ref.shape
    nrows = cz * cy
    row_iota = lax.broadcasted_iota(jnp.int32, (nmark, nrows), 1)
    lane_iota = lax.broadcasted_iota(jnp.int32, (nmark, cx), 1)
    cells = jnp.transpose(cell_ref[...], (1, 0))
    weights = jnp.transpose(weight_ref[...], (1, 0))
    for k in range(kk):
        cell = cells[:, k : k + 1]
        line = cell // cx
        block = pl.ds(k * nmark, nmark)
        picked = jnp.where(row_iota == line, 1.0, 0.0).astype(jnp.bfloat16)
        pick[block, 0:nrows] = picked
        pick[block, nrows : 2 * nrows] = picked
        lanes[block, :] = jnp.where(lane_iota == cell - line * cx, weights[:, k : k + 1], 0.0)
    ids = jnp.broadcast_to(seg_ref[...].reshape(1, nmark), (8, nmark))
    ids = jnp.transpose(ids, (1, 0))[:, 0:1]
    lane_count = SEG_DEV * ng2
    seg_iota = lax.broadcasted_iota(jnp.int32, (nmark, lane_count), 1)
    for j in range(ng1):
        hot[:, j * lane_count : (j + 1) * lane_count] = jnp.where(
            seg_iota == ids - j * lane_count, 1.0, 0.0
        ).astype(jnp.bfloat16)

    for_others(z, nz, lambda k, j: d2_copy(k, j, j).wait_recv())
    total = d2[0]
    for j in range(1, nz):
        total = total + d2[j]
    d1s[xc] = total
    eddy_rows = jnp.maximum(d1s[xc, 0:rows, :] / (d1s[xc, rows : 2 * rows, :] + eps_sum), 0.0)
    d3[xc] = eddy_rows
    for_others(xc, nxc, lambda k, j: d3_copy(k, j, xc).start())

    @pl.when(last)
    def _():
        for_all(nxc, lambda j: edge_copy(j, 0).start())

    @pl.when(first)
    def _():
        for_all(nxc, lambda j: edge_copy(j, 1).start())

    for copy in halo:
        copy.wait()
    for_others(xc, nxc, lambda k, j: d3_copy(k, j, j).wait_recv())
    for side in range(2):
        edge_copy(0, side).wait_recv()
    for j in range(nxc):
        eddy_ref[j * rows : (j + 1) * rows, :] = d3[j]
        eddyx[ROW + j * rows : ROW + (j + 1) * rows, :] = d3[j]
    eddyx[ROW - 1 : ROW, :] = dlow[rows - 1 : rows, :]
    eddyx[ROW + cy : ROW + cy + 1, :] = dhigh[0:1, :]

    def relax(p, start, count, which):
        here = pl.ds(start, count)
        mag = mags[p, pl.ds(start - ROW + 1, count), :]
        rate = 1.0 / (0.5 + 3.0 * (base_visc + eddyx[here, :] * mag))
        parts = {}

        def moment(n):
            if n not in parts:
                parts[n] = rate * shear[n, p, here, :]
            return parts[n]

        def lost(n):
            if n in parts:
                return parts[n]
            if n == "y":
                value = moment(XX) + moment(WW)
            elif n == "z":
                value = moment(XX) - moment(WW)
            else:
                value = -2.0 * moment(XX)
            parts[n] = value
            return value

        rules = [
            lambda: 2.0 * moment(XX),
            lambda: moment(WW) - moment(XX),
            lambda: -lost("y"),
            lambda: lost("y") + moment(XY),
            lambda: lost("y") - moment(XY),
            lambda: lost("z") + moment(XZ),
            lambda: lost("z") - moment(XZ),
            lambda: lost("yz") + moment(YZ),
            lambda: lost("yz") - moment(YZ),
        ]
        for q in which:
            value = post[PLACE[q], p, here, :]
            if q:
                pair = (q - 1) // 2
                if ("pair", pair) not in parts:
                    parts["pair", pair] = rules[pair]()
                value = value - parts["pair", pair]
            post[PLACE[q], p, here, :] = value.astype(jnp.bfloat16).astype(jnp.float32)

    def going(dz, dy):
        return [
            q
            for q, (ex, ey, ez) in enumerate(VELOCITIES)
            if (dz == 0 or ez == dz) and (dy == 0 or ey == dy)
        ]

    def finish_plane(i, carry):
        relax(i, ROW, cy, range(19))
        relax(i, ROW - 1, 1, going(0, 1))
        relax(i, ROW + cy, 1, going(0, -1))
        return carry

    lax.fori_loop(1, cz + 1, finish_plane, 0, unroll=2)
    for p, dz in ((0, 1), (cz + 1, -1)):
        relax(p, ROW, cy, going(dz, 0))
        relax(p, ROW - 1, 1, going(dz, 1))
        relax(p, ROW + cy, 1, going(dz, -1))

    def momentum_plane(i, carry):
        def came(q):
            ex, ey, ez = VELOCITIES[q]
            return post[PLACE[q], i + 1 - ez, pl.ds(ROW - ey, cy), :]

        up = {q: came(q) for q in (1, 7, 9, 11, 13)}
        down = {q: came(q) for q in (2, 8, 10, 12, 14)}
        east = (up[1] + up[7] + up[9] + up[11] + up[13], up[7] - up[9], up[11] - up[13])
        west = (
            down[2] + down[8] + down[10] + down[12] + down[14],
            down[10] - down[8],
            down[14] - down[12],
        )
        d56, d78 = came(15) - came(16), came(17) - came(18)
        jx = roll_x(east[0], 1) - roll_x(west[0], -1)
        jy = (came(3) - came(4)) + (d56 + d78) + (roll_x(east[1], 1) + roll_x(west[1], -1))
        jz = (came(5) - came(6)) + (d56 - d78) + (roll_x(east[2], 1) + roll_x(west[2], -1))
        lines = pl.ds(pl.multiple_of(i * cy, cy), cy)
        lower = pl.ds(pl.multiple_of(nrows + i * cy, cy), cy)
        for n, value in enumerate((jx, jy, jz)):
            high = value.astype(jnp.bfloat16)
            low = (value - high.astype(jnp.float32)).astype(jnp.bfloat16)
            mom[lines, n * cx : (n + 1) * cx] = high
            mom[lower, n * cx : (n + 1) * cx] = low
        return carry

    lax.fori_loop(0, cz, momentum_plane, 0, unroll=2)

    gath[...] = jnp.dot(pick[...], mom[...], preferred_element_type=jnp.float32)

    def parts_of(value):
        first_part = value.astype(jnp.bfloat16)
        return first_part, (value - first_part.astype(jnp.float32)).astype(jnp.bfloat16)

    def dot_t(a, b):
        return lax.dot_general(a, b, (((1,), (1,)), ((), ())), preferred_element_type=jnp.float32)

    ones = jnp.ones((16, cx), jnp.bfloat16)
    forces = []
    for n in range(3):
        acc = None
        for k in range(kk):
            block = pl.ds(k * nmark, nmark)
            term = lanes[block, :] * gath[block, n * cx : (n + 1) * cx]
            acc = term if acc is None else acc + term
        a, b = parts_of(acc)
        forces.append(-(dot_t(ones, a) + dot_t(ones, b))[0:8])
    which = lax.broadcasted_iota(jnp.int32, (8, nmark), 0)
    force = jnp.where(which == 0, forces[0], jnp.where(which == 1, forces[1], forces[2]))
    a, b = parts_of(force)
    both = jnp.concatenate([a.astype(jnp.float32), b.astype(jnp.float32)], axis=0).astype(jnp.bfloat16)
    sums_of = jnp.dot(both, hot[...], preferred_element_type=jnp.float32)
    sums_of = sums_of[0:3] + sums_of[8:11]
    for j in range(ng1):
        h1s[j] = sums_of[:, j * lane_count : (j + 1) * lane_count]

    for_others(g1, ng1, lambda k, j: h1_copy(k, j, g1).start())
    h1r[g1] = h1s[g1]

    def stream_plane(i, carry):
        for q, (ex, ey, ez) in enumerate(VELOCITIES):
            value = post[PLACE[q], i + 1 - ez, pl.ds(ROW - ey, cy), :]
            if ex:
                value = roll_x(value, ex)
            outv[q, i] = value.astype(jnp.bfloat16)
        return carry

    lax.fori_loop(0, cz, stream_plane, 0)
    for_others(g1, ng1, lambda k, j: h1_copy(k, j, j).wait_recv())
    total = h1r[0]
    for j in range(1, ng1):
        total = total + h1r[j]
    h2[g2] = total
    for_others(g2, ng2, lambda k, j: h2_copy(k, j, g2).start())

    for_others(xc, nxc, lambda k, j: d1_copy(k, j, xc).wait_send())
    for_others(z, nz, lambda k, j: d2_copy(k, j, z).wait_send())
    for_others(xc, nxc, lambda k, j: d3_copy(k, j, xc).wait_send())
    for_others(g1, ng1, lambda k, j: h1_copy(k, j, g1).wait_send())

    @pl.when(last)
    def _():
        for_all(nxc, lambda j: edge_copy(j, 0).wait_send())

    @pl.when(first)
    def _():
        for_all(nxc, lambda j: edge_copy(j, 1).wait_send())

    for_others(g2, ng2, lambda k, j: h2_copy(k, j, j).wait_recv())
    total = h2[0]
    for j in range(1, ng2):
        total = total + h2[j]
    mine = pltpu.roll(total, (lane_count - place * SEG_DEV) % lane_count, axis=1)
    force_ref[...] = mine[:, 0:SEG_DEV]
    for_others(g2, ng2, lambda k, j: h2_copy(k, j, g2).wait_send())


def write_kernel(outv, eddy, force, out_hbm, eddy_hbm, force_hbm, sem):
    pieces = sem.shape[0] - 2
    step = -(-outv.shape[0] // pieces)
    copies = []
    for i in range(pieces):
        some = pl.ds(i * step, min(step, outv.shape[0] - i * step))
        copies.append(pltpu.make_async_copy(outv.at[some], out_hbm.at[some], sem.at[i]))
    copies.append(pltpu.make_async_copy(eddy, eddy_hbm, sem.at[pieces]))
    copies.append(pltpu.make_async_copy(force, force_hbm, sem.at[pieces + 1]))
    for copy in copies:
        copy.start()
    for copy in copies:
        copy.wait()


def local(split, populations, cell_index, marker_weight, segment_id):
    nq, cz, cy, cx = populations.shape
    nmark, kk = cell_index.shape
    nz, nx, nc, ny = split
    nxc = nx * nc
    ng1, ng2 = nz * (nx // 2), 2 * nc * ny
    rows = cy // nxc
    f32, bf16 = jnp.float32, jnp.bfloat16
    dma = pltpu.SemaphoreType.DMA
    vmem = pl.BlockSpec(memory_space=pltpu.VMEM)
    hbm = pl.BlockSpec(memory_space=pltpu.HBM)
    lane_count = SEG_DEV * ng2
    velocity, pops = pl.pallas_call(
        functools.partial(velocity_kernel, split),
        out_shape=(
            pltpu.VMEM((3, cz + 4, TOP, cx), f32),
            pltpu.VMEM((nq, cz, cy, cx), bf16),
        ),
        in_specs=[hbm],
        out_specs=(vmem, vmem),
        scratch_shapes=[
            dma((4,)),
            dma((8,)),
            dma((8,)),
        ],
        compiler_params=pltpu.CompilerParams(
            collective_id=0, has_side_effects=True, vmem_limit_bytes=8 * 1024 * 1024
        ),
    )(pltpu.with_memory_space_constraint(populations, pltpu.HBM))
    scratch = [
        pltpu.VMEM((3 * cx, cx), bf16),
        pltpu.VMEM((12, cy, cx), f32),
        pltpu.VMEM((12, cy, cx), f32),
        pltpu.VMEM((cz + 2, 40, cx), f32),
        pltpu.VMEM((12, 40, cx), f32),
        pltpu.VMEM((12, 40, cx), f32),
        pltpu.VMEM((3, 48, cx), f32),
        pltpu.VMEM((3, 48, cx), f32),
        pltpu.VMEM((3, cz + 3, 40, cx), f32),
        pltpu.VMEM((12, cz + 4, cy, cx), f32),
        pltpu.VMEM((2, cy, cx), f32),
        pltpu.VMEM((5, cz + 2, TOP, cx), f32),
        pltpu.VMEM((nq, cz + 2, TOP, cx), f32),
        pltpu.VMEM((TOP, cx), f32),
        pltpu.VMEM((2 * cz * cy, 3 * cx), bf16),
        pltpu.VMEM((kk * nmark, 2 * cz * cy), bf16),
        pltpu.VMEM((kk * nmark, cx), f32),
        pltpu.VMEM((kk * nmark, 3 * cx), f32),
        pltpu.VMEM((nmark, ng1 * lane_count), bf16),
        pltpu.VMEM((nxc, 2 * rows, cx), f32),
        pltpu.VMEM((nxc, 2 * rows, cx), f32),
        pltpu.VMEM((nz, 2 * rows, cx), f32),
        pltpu.VMEM((nxc, rows, cx), f32),
        pltpu.VMEM((rows, cx), f32),
        pltpu.VMEM((rows, cx), f32),
        pltpu.VMEM((ng1, 3, lane_count), f32),
        pltpu.VMEM((ng1, 3, lane_count), f32),
        pltpu.VMEM((ng2, 3, lane_count), f32),
        dma((9,)),
        dma((9,)),
        dma((8,)),
        dma((8,)),
        dma((nxc,)),
        dma((nxc,)),
        dma((nz,)),
        dma((nz,)),
        dma((nxc,)),
        dma((nxc,)),
        dma((2, nxc)),
        dma((2,)),
        dma((ng1,)),
        dma((ng1,)),
        dma((ng2,)),
        dma((ng2,)),
    ]
    results = pl.pallas_call(
        functools.partial(step_kernel, split),
        out_shape=(
            pltpu.VMEM((nq, cz, cy, cx), bf16),
            pltpu.VMEM((cy, cx), f32),
            pltpu.VMEM((3, SEG_DEV), f32),
        ),
        in_specs=[vmem, vmem, vmem, vmem, vmem],
        out_specs=(vmem, vmem, vmem),
        scratch_shapes=scratch,
        compiler_params=pltpu.CompilerParams(
            collective_id=1, has_side_effects=True, vmem_limit_bytes=40 * 1024 * 1024
        ),
    )(velocity, pops, cell_index.T, marker_weight.T, segment_id)
    return pl.pallas_call(
        write_kernel,
        out_shape=(
            jax.ShapeDtypeStruct((nq, cz, cy, cx), bf16),
            jax.ShapeDtypeStruct((cy, cx), f32),
            jax.ShapeDtypeStruct((3, SEG_DEV), f32),
        ),
        in_specs=[vmem, vmem, vmem],
        out_specs=(hbm, hbm, hbm),
        scratch_shapes=[dma((6,))],
        compiler_params=pltpu.CompilerParams(vmem_limit_bytes=1024 * 1024),
    )(*results)


def solution(mesh):
    in_specs = (
        P(None, "span", "cross", None),
        P(("span", "cross"), None),
        P(("span", "cross"), None),
        P(("span", "cross")),
    )
    out_specs = (P(None, "span", "cross", None), P("cross", None), P(None, ("span", "cross")))
    sizes = dict(mesh.shape)
    split = (sizes["span"] // (CHIPS_X * CORES), CHIPS_X, CORES, sizes["cross"])
    return jax.shard_map(
        functools.partial(local, split),
        mesh=mesh,
        in_specs=in_specs,
        out_specs=out_specs,
        check_vma=False,
    )
```

```python
import functools

import jax
import jax.numpy as jnp
from jax import lax
from jax.experimental import pallas as pl
from jax.experimental.pallas import tpu as pltpu
from jax.sharding import PartitionSpec as P

SEG_DEV = 8
MESH = pl.DeviceIdType.MESH
eps_sum = 1e-06
base_visc = 0.005

CHIPS_X = 4
CORES = 2

VELOCITIES = [
    (0, 0, 0),
    (1, 0, 0),
    (-1, 0, 0),
    (0, 1, 0),
    (0, -1, 0),
    (0, 0, 1),
    (0, 0, -1),
    (1, 1, 0),
    (-1, -1, 0),
    (1, -1, 0),
    (-1, 1, 0),
    (1, 0, 1),
    (-1, 0, -1),
    (1, 0, -1),
    (-1, 0, 1),
    (0, 1, 1),
    (0, -1, -1),
    (0, 1, -1),
    (0, -1, 1),
]
ORDER = [18, 5, 11, 14, 15, 3, 7, 10, 17, 6, 12, 13, 16, 4, 8, 9, 0, 1, 2]
PLACE = [ORDER.index(q) for q in range(19)]

ROW = 8
TOP = 48


def add_pairs(f):
    s = [f[2 * i + 1] + f[2 * i + 2] for i in range(9)]
    d = [f[2 * i + 1] - f[2 * i + 2] for i in range(9)]
    return s, d


def tri(low, mid, high):
    return (low + high) + (mid + mid)


def roll_x(a, shift):
    return pltpu.roll(a, shift % a.shape[-1], axis=a.ndim - 1)


def strain_of(d):
    exy, exz, eyz = d[0][1] + d[1][0], d[0][2] + d[2][0], d[1][2] + d[2][1]
    diag = d[0][0] * d[0][0] + d[1][1] * d[1][1] + d[2][2] * d[2][2]
    off = exy * exy + exz * exz + eyz * eyz
    mag = jnp.sqrt(0.5 * diag + 0.25 * off)
    return (d[0][0], d[1][1], d[2][2], exy, exz, eyz), mag


PAIRS = [(0, 0), (1, 1), (2, 2), (0, 1), (0, 2), (1, 2)]


SIDES = [(1, 0), (-1, 0), (0, 1), (0, -1), (1, 1), (1, -1), (-1, 1), (-1, -1)]
XZ, XX, WW, YZ, XY = range(5)


def near(split, dz, dy):
    nz, nx, nc, ny = split
    nspan = nz * nx * nc
    s, y = lax.axis_index("span"), lax.axis_index("cross")
    return ((s + dz + nspan) % nspan, (y + dy + ny) % ny)


def ranges(d, first, size, width):
    if d == 0:
        return pl.ds(first, size), pl.ds(first, size)
    if d > 0:
        return pl.ds(first + size - width, width), pl.ds(first - width, width)
    return pl.ds(first, width), pl.ds(first + size, width)


def velocity_kernel(split, pops_hbm, vel, pops, in_sem, v_send, v_recv):
    cz, cy, cx = pops.shape[1:]
    nchunk = in_sem.shape[0]
    step = cz // nchunk

    def fetch(i):
        some = pl.ds(i * step, step)
        return pltpu.make_async_copy(pops_hbm.at[:, some], pops.at[:, some], in_sem.at[i])

    order = [0, nchunk - 1] + list(range(1, nchunk - 1))
    for i in order:
        fetch(i).start()
    barrier = pltpu.get_barrier_semaphore()
    for dz, dy in SIDES:
        pl.semaphore_signal(
            barrier, inc=1, device_id=near(split, dz, dy), device_id_type=MESH
        )

    def moments_plane(i, carry):
        f = [pops[q, i].astype(jnp.float32) for q in range(19)]
        sm, d = add_pairs(f)
        density = f[0] + ((sm[0] + sm[1] + sm[2]) + (sm[3] + sm[4] + sm[5]) + (sm[6] + sm[7] + sm[8]))
        jx = d[0] + (d[3] + d[4]) + (d[5] + d[6])
        jy = d[1] + (d[3] - d[4]) + (d[7] + d[8])
        jz = d[2] + (d[5] - d[6]) + (d[7] - d[8])
        inv = 1.0 / density
        inner = pl.ds(ROW, cy)
        vel[0, i + 2, inner, :] = jx * inv
        vel[1, i + 2, inner, :] = jy * inv
        vel[2, i + 2, inner, :] = jz * inv
        return carry

    def moments_of(i):
        fetch(i).wait()
        lax.fori_loop(i * step, (i + 1) * step, moments_plane, 0)

    def vel_copy(i):
        dz, dy = SIDES[i]
        zs, zt = ranges(dz, 2, cz, 2)
        ys, yt = ranges(dy, ROW, cy, 2)
        return pltpu.make_async_remote_copy(
            src_ref=vel.at[:, zs, ys, :],
            dst_ref=vel.at[:, zt, yt, :],
            send_sem=v_send.at[i],
            recv_sem=v_recv.at[i],
            device_id=near(split, dz, dy),
            device_id_type=MESH,
        )

    for i in order[:2]:
        moments_of(i)
    pl.semaphore_wait(barrier, len(SIDES))
    for i, (dz, dy) in enumerate(SIDES):
        if dz:
            vel_copy(i).start()
    for i in order[2:]:
        moments_of(i)
    for i, (dz, dy) in enumerate(SIDES):
        if not dz:
            vel_copy(i).start()
    for i in range(len(SIDES)):
        vel_copy(i).wait()


def step_kernel(
    split,
    vel,
    pops,
    cell_ref,
    weight_ref,
    seg_ref,
    outv,
    eddy_ref,
    force_ref,
    smoother,
    hats_a,
    hats_b,
    mags,
    tmp_a,
    tmp_b,
    vtmp_a,
    vtmp_b,
    vhat,
    filt,
    sums,
    shear,
    post,
    eddyx,
    mom,
    pick,
    lanes,
    gath,
    hot,
    d1s,
    d1r,
    d2,
    d3,
    dlow,
    dhigh,
    h1s,
    h1r,
    h2,
    p_send,
    p_recv,
    s_send,
    s_recv,
    d1_sem,
    d2_sem,
    d3_sem,
    e_send,
    e_recv,
    h1_sem,
    h2_sem,
):
    nz, nx, nc, ny = split
    nxc = nx * nc
    cz, cy, cx = pops.shape[1:]
    half = nx // 2
    ng1, ng2 = nz * half, 2 * nc * ny
    s = lax.axis_index("span")
    y = lax.axis_index("cross")
    z, xc = s // nxc, s % nxc
    x, c = xc // nc, xc % nc
    g1 = z * half + x // 2
    g2 = y * (2 * nc) + (x % 2) * nc + c
    place = (x % 2) * (nc * ny) + c * ny + y
    y_up, y_down = (y + 1) % ny, (y + ny - 1) % ny

    def xc_dev(k):
        return (s - xc + (xc + k) % nxc, y)

    def z_dev(k):
        return ((s + nxc * k) % (nz * nxc), y)

    def g1_dev(k):
        return ((s + 2 * nc * k) % (nz * nxc), y)

    def g2_dev(k):
        other = (g2 + k) % ng2
        return (s - s % (2 * nc) + other % (2 * nc), other // (2 * nc))

    def for_others(me, count, act):
        for k in sorted(range(1, count), key=lambda k: abs(2 * k - count)):
            act(k, (me + k) % count)

    def for_all(count, act):
        def body(j, carry):
            act(j)
            return carry

        lax.fori_loop(0, count, body, 0)

    barrier = pltpu.get_barrier_semaphore()

    def greet(dev):
        pl.semaphore_signal(barrier, inc=1, device_id=dev, device_id_type=MESH)

    for_others(g1, ng1, lambda k, j: greet(g1_dev(k)))
    for_others(g2, ng2, lambda k, j: greet(g2_dev(k)))
    for_others(z, nz, lambda k, j: greet(z_dev(k)))
    for_others(xc, nxc, lambda k, j: greet(xc_dev(k)))
    for dz, dy in SIDES:
        greet(near(split, dz, dy))
    greet((z * nxc + nxc - 1, y_down))
    greet((z * nxc, y_up))
    last, first = xc == nxc - 1, xc == 0
    greeted = len(SIDES) + (nxc - 1) + (nz - 1) + (ng1 - 1) + (ng2 - 1)
    greeted = greeted + jnp.where(jnp.logical_or(last, first), nxc, 0)

    apart = lax.broadcasted_iota(jnp.int32, (cx, cx), 0) - lax.broadcasted_iota(jnp.int32, (cx, cx), 1)
    apart = (apart + cx) % cx
    beside = jnp.logical_or(apart == 1, apart == cx - 1)
    circulant = jnp.where(apart == 0, 2.0, jnp.where(beside, 1.0, 0.0)).astype(jnp.bfloat16)
    for n in range(3):
        smoother[n * cx : (n + 1) * cx, :] = circulant

    def smooth_x(values):
        both = jnp.concatenate(values, axis=0)
        high = both.astype(jnp.bfloat16)
        rest = both - high.astype(jnp.float32)
        mid = rest.astype(jnp.bfloat16)
        low = (rest - mid.astype(jnp.float32)).astype(jnp.bfloat16)
        parts = jnp.concatenate([high, mid, low], axis=1)
        return jnp.dot(parts, smoother[...], preferred_element_type=jnp.float32)

    def products(p, tmp, vtmp):
        mid, low, high = pl.ds(ROW - 1, 40), pl.ds(ROW - 2, 40), pl.ds(ROW, 40)
        v = [vel[a, p + 1, mid, :] for a in range(3)]
        for n, (a, b) in enumerate(PAIRS):
            tmp[n + 6] = v[a] * v[b]
        d = []
        for a in range(3):
            below = vel[a, p + 1, low, :]
            vtmp[a, 0:40, :] = tri(vel[a, p, low, :], below, vel[a, p + 2, low, :])
            dx = roll_x(v[a], -1) - roll_x(v[a], 1)
            dy = vel[a, p + 1, high, :] - below
            dz = vel[a, p + 2, mid, :] - vel[a, p, mid, :]
            d.append((dx, dy, dz))
        e, mag = strain_of(d)
        mags[p] = mag
        half_mag = 0.5 * mag
        for n in range(3):
            tmp[n] = mag * e[n]
            tmp[n + 3] = half_mag * e[n + 3]

    def filters(p, tmp, vtmp):
        for n in range(12):
            filt[n, p + 1] = tri(tmp[n, 0:cy, :], tmp[n, 1 : cy + 1, :], tmp[n, 2 : cy + 2, :])
        along_y = [tri(vtmp[a, 0:40, :], vtmp[a, 1:41, :], vtmp[a, 2:42, :]) for a in range(3)]
        smoothed = smooth_x(along_y)
        for a in range(3):
            vhat[a, p + 1] = (1.0 / 64.0) * smoothed[a * 40 : (a + 1) * 40]

    def two_planes(i, carry):
        products(2 * i, tmp_a, vtmp_a)
        filters(2 * i - 1, tmp_b, vtmp_b)
        products(2 * i + 1, tmp_b, vtmp_b)
        filters(2 * i, tmp_a, vtmp_a)
        return carry

    lax.fori_loop(0, (cz + 2) // 2, two_planes, 0)
    filters(cz + 1, tmp_b, vtmp_b)

    def hats_of(i, hats):
        along_z = [tri(filt[n, i + 1], filt[n, i + 2], filt[n, i + 3]) for n in range(12)]
        smoothed = smooth_x(along_z)
        for n in range(12):
            hats[n] = (1.0 / 64.0) * smoothed[n * cy : (n + 1) * cy]

    def add_plane(i, hats, plane_lm, plane_mm):
        mid, low, high = pl.ds(1, cy), pl.ds(0, cy), pl.ds(2, cy)
        v = [vhat[a, i + 2, mid, :] for a in range(3)]
        d = []
        for a in range(3):
            dx = roll_x(v[a], -1) - roll_x(v[a], 1)
            dy = vhat[a, i + 2, high, :] - vhat[a, i + 2, low, :]
            dz = vhat[a, i + 3, mid, :] - vhat[a, i + 1, mid, :]
            d.append((dx, dy, dz))
        e, mag = strain_of(d)
        four, two = 4.0 * mag, 2.0 * mag
        lm = mm = lm_off = mm_off = None
        for n, (a, b) in enumerate(PAIRS):
            model = hats[n] - (four if n < 3 else two) * e[n]
            leonard = hats[n + 6] - v[a] * v[b]
            if n == 0:
                lm, mm = leonard * model, model * model
            elif n < 3:
                lm, mm = lm + leonard * model, mm + model * model
            elif n == 3:
                lm_off, mm_off = leonard * model, model * model
            else:
                lm_off, mm_off = lm_off + leonard * model, mm_off + model * model
        return plane_lm + (lm + 2.0 * lm_off), plane_mm + (mm + 2.0 * mm_off)

    def second_pass(i, carry):
        hats_of(2 * i + 1, hats_b)
        carry = add_plane(2 * i, hats_a, *carry)
        hats_of(2 * i + 2, hats_a)
        return add_plane(2 * i + 1, hats_b, *carry)

    zero = jnp.zeros((cy, cx), jnp.float32)
    hats_of(0, hats_a)
    plane_lm, plane_mm = lax.fori_loop(0, cz // 2, second_pass, (zero, zero))

    rows = cy // nxc
    sums[0] = plane_lm
    sums[1] = plane_mm
    for j in range(nxc):
        d1s[j, 0:rows, :] = sums[0, j * rows : (j + 1) * rows, :]
        d1s[j, rows : 2 * rows, :] = sums[1, j * rows : (j + 1) * rows, :]

    class Exchange:
        def __init__(self, src, dst, me, count, dev, sems, own):
            self.src, self.dst, self.me, self.count, self.dev = src, dst, me, count, dev
            self.sems, self.own = sems, own

        def copy(self, src, dst, k):
            return pltpu.make_async_remote_copy(
                src_ref=src,
                dst_ref=dst,
                send_sem=self.sems.at[0],
                recv_sem=self.sems.at[1],
                device_id=self.dev(k),
                device_id_type=MESH,
            )

        def start(self):
            def send(k, j):
                self.copy(self.src.at[self.me if self.own else j], self.dst.at[self.me], k).start()

            for_others(self.me, self.count, send)

        def all_of(self):
            some = pl.ds(0, self.count - 1)
            return self.copy(self.src.at[some], self.dst.at[some], 1)

    d1x = Exchange(d1s, d1r, xc, nxc, xc_dev, d1_sem, False)
    d2x = Exchange(d2, d2, z, nz, z_dev, d2_sem, True)
    d3x = Exchange(d3, d3, xc, nxc, xc_dev, d3_sem, True)
    h1x = Exchange(h1s, h1r, g1, ng1, g1_dev, h1_sem, False)
    h2x = Exchange(h2, h2, g2, ng2, g2_dev, h2_sem, True)

    def edge_copy(j, side):
        return pltpu.make_async_remote_copy(
            src_ref=d3.at[xc],
            dst_ref=dlow if side == 0 else dhigh,
            send_sem=e_send.at[side],
            recv_sem=e_recv.at[side],
            device_id=(z * nxc + j, y_up if side == 0 else y_down),
            device_id_type=MESH,
        )

    def edges_sent(side):
        pltpu.make_async_remote_copy(
            src_ref=d3,
            dst_ref=d3,
            send_sem=e_send.at[side],
            recv_sem=e_recv.at[side],
            device_id=(z * nxc, y_up),
            device_id_type=MESH,
        ).wait_send()

    pl.semaphore_wait(barrier, greeted)
    d1x.start()

    inner = pl.ds(ROW, cy)

    def collide_plane(i, carry):
        f = [pops[q, i].astype(jnp.float32) for q in range(19)]
        sm, d = add_pairs(f)
        sx, sy, sz, sa, sb, sc, sd, se, sg = sm
        dx, dy, dz, da, db, dc, dd, de, dg = d
        ux, uy, uz = [vel[a, i + 2, inner, :] for a in range(3)]
        xy, xz, yz = sa + sb, sc + sd, se + sg
        axis, diag = sx + sy + sz, xy + xz + yz
        abp, abm, cdp, cdm, egp, egm = da + db, da - db, dc + dd, dc - dd, de + dg, de - dg
        jx, jy, jz = dx + (abp + cdp), dy + (abm + egp), dz + (cdm + egm)
        jxx, jyy, jzz = jx * ux, jy * uy, jz * uz
        ju = jxx + jyy + jzz
        ne = (1.19 * 19.0 / 2394.0) * (diag - f[0] - ju)
        neps = (1.4 / 252.0) * (9.0 * f[0] - 7.0 * axis - 2.0 * diag + 5.5 * ju)
        ax_part = -11.0 * ne - 4.0 * neps
        dg_part = 8.0 * ne + neps
        eq_xx = 3.0 * jxx - ju
        eq_ww = jyy - jzz
        axis_xx, diag_xx = 3.0 * sx - axis, diag - 3.0 * yz
        axis_ww, diag_ww = sy - sz, xy - xz
        pi_xx = (1.4 / 72.0) * (diag_xx - 2.0 * axis_xx + 0.5 * eq_xx)
        pi_ww = (1.4 / 24.0) * (diag_ww - 2.0 * axis_ww + 0.5 * eq_ww)
        shear[XX, i + 1, inner, :] = (1.0 / 36.0) * (axis_xx + diag_xx - eq_xx)
        shear[WW, i + 1, inner, :] = (1.0 / 12.0) * (axis_ww + diag_ww - eq_ww)
        shear[XY, i + 1, inner, :] = 0.25 * (sa - sb - jx * uy)
        shear[XZ, i + 1, inner, :] = 0.25 * (sc - sd - jx * uz)
        shear[YZ, i + 1, inner, :] = 0.25 * (se - sg - jy * uz)
        two_xx, two_ww = 2.0 * pi_xx, 2.0 * pi_ww
        base_yz = ax_part + two_xx
        hx = ax_part - 2.0 * two_xx
        hy, hz = base_yz - two_ww, base_yz + two_ww
        base_d = dg_part + pi_xx
        hxy, hxz, hyz = base_d + pi_ww, base_d - pi_ww, dg_part - two_xx
        tx = (1.2 / 8.0) * ((1.0 / 3.0) * jx - dx)
        ty = (1.2 / 8.0) * ((1.0 / 3.0) * jy - dy)
        tz = (1.2 / 8.0) * ((1.0 / 3.0) * jz - dz)
        mx = (1.98 / 8.0) * (abp - cdp)
        my = (1.98 / 8.0) * (egp - abm)
        mz = (1.98 / 8.0) * (cdm - egm)
        xp, xm, yp, ym, zp, zm = tx + mx, tx - mx, ty + my, ty - my, tz + mz, tz - mz
        halves = [
            (hx, -4.0 * tx),
            (hy, -4.0 * ty),
            (hz, -4.0 * tz),
            (hxy, xp + ym),
            (hxy, xp - ym),
            (hxz, xm + zp),
            (hxz, xm - zp),
            (hyz, yp + zm),
            (hyz, yp - zm),
        ]
        post[PLACE[0], i + 1, inner, :] = f[0] + (30.0 * ne - 12.0 * neps)
        for n, (even, odd) in enumerate(halves):
            post[PLACE[2 * n + 1], i + 1, inner, :] = f[2 * n + 1] - (even + odd)
            post[PLACE[2 * n + 2], i + 1, inner, :] = f[2 * n + 2] - (even - odd)
        return carry

    lax.fori_loop(0, cz, collide_plane, 0)

    crossing = [
        ((1, 0), 0, 5),
        ((-1, 0), 8, 5),
        ((0, 1), 4, 5),
        ((0, -1), 12, 4),
        ((0, -1), 0, 1),
        ((1, 1), 4, 1),
        ((1, -1), 0, 1),
        ((-1, 1), 8, 1),
        ((-1, -1), 12, 1),
    ]

    def halo_copy(ref, side, first_of, count, send, recv):
        dz, dy = side
        zs, zt = ranges(dz, 1, cz, 1)
        ys, yt = ranges(dy, ROW, cy, 1)
        group = pl.ds(first_of, count)
        return pltpu.make_async_remote_copy(
            src_ref=ref.at[group, zs, ys, :],
            dst_ref=ref.at[group, zt, yt, :],
            send_sem=send,
            recv_sem=recv,
            device_id=near(split, dz, dy),
            device_id_type=MESH,
        )

    halo = []
    for i, (side, first_of, count) in enumerate(crossing):
        halo.append(halo_copy(post, side, first_of, count, p_send.at[i], p_recv.at[i]))
    for i, side in enumerate(SIDES):
        first_of = 0 if side[1] == 0 else (1 if side[0] == 0 else 1)
        count = 3 if side[0] and side[1] else 4
        halo.append(halo_copy(shear, side, first_of, count, s_send.at[i], s_recv.at[i]))

    for copy in halo:
        copy.start()

    d1r[xc] = d1s[xc]
    d1x.all_of().wait_recv()
    total = d1r[0]
    for j in range(1, nxc):
        total = total + d1r[j]
    d2[z] = total
    d2x.start()

    kk, nmark = cell_ref.shape
    nrows = cz * cy
    row_iota = lax.broadcasted_iota(jnp.int32, (nmark, nrows), 1)
    lane_iota = lax.broadcasted_iota(jnp.int32, (nmark, cx), 1)
    cells = jnp.transpose(cell_ref[...], (1, 0))
    weights = jnp.transpose(weight_ref[...], (1, 0))
    for k in range(kk):
        cell = cells[:, k : k + 1]
        line = cell // cx
        block = pl.ds(k * nmark, nmark)
        picked = jnp.where(row_iota == line, 1.0, 0.0).astype(jnp.bfloat16)
        pick[block, 0:nrows] = picked
        pick[block, nrows : 2 * nrows] = picked
        lanes[block, :] = jnp.where(lane_iota == cell - line * cx, weights[:, k : k + 1], 0.0)
    ids = jnp.broadcast_to(seg_ref[...].reshape(1, nmark), (8, nmark))
    ids = jnp.transpose(ids, (1, 0))[:, 0:1]
    lane_count = SEG_DEV * ng2
    seg_iota = lax.broadcasted_iota(jnp.int32, (nmark, lane_count), 1)
    for j in range(ng1):
        hot[:, j * lane_count : (j + 1) * lane_count] = jnp.where(
            seg_iota == ids - j * lane_count, 1.0, 0.0
        ).astype(jnp.bfloat16)

    d2x.all_of().wait_recv()
    total = d2[0]
    for j in range(1, nz):
        total = total + d2[j]
    d1s[xc] = total
    eddy_rows = jnp.maximum(d1s[xc, 0:rows, :] / (d1s[xc, rows : 2 * rows, :] + eps_sum), 0.0)
    d3[xc] = eddy_rows
    d3x.start()

    @pl.when(last)
    def _():
        for_all(nxc, lambda j: edge_copy(j, 0).start())

    @pl.when(first)
    def _():
        for_all(nxc, lambda j: edge_copy(j, 1).start())

    for copy in halo:
        copy.wait()
    d3x.all_of().wait_recv()
    for side in range(2):
        edge_copy(0, side).wait_recv()
    for j in range(nxc):
        eddy_ref[j * rows : (j + 1) * rows, :] = d3[j]
        eddyx[ROW + j * rows : ROW + (j + 1) * rows, :] = d3[j]
    eddyx[ROW - 1 : ROW, :] = dlow[rows - 1 : rows, :]
    eddyx[ROW + cy : ROW + cy + 1, :] = dhigh[0:1, :]

    def relax(p, start, count, which):
        here = pl.ds(start, count)
        mag = mags[p, pl.ds(start - ROW + 1, count), :]
        rate = 1.0 / (0.5 + 3.0 * (base_visc + eddyx[here, :] * mag))
        parts = {}

        def moment(n):
            if n not in parts:
                parts[n] = rate * shear[n, p, here, :]
            return parts[n]

        def lost(n):
            if n in parts:
                return parts[n]
            if n == "y":
                value = moment(XX) + moment(WW)
            elif n == "z":
                value = moment(XX) - moment(WW)
            else:
                value = -2.0 * moment(XX)
            parts[n] = value
            return value

        rules = [
            lambda: 2.0 * moment(XX),
            lambda: moment(WW) - moment(XX),
            lambda: -lost("y"),
            lambda: lost("y") + moment(XY),
            lambda: lost("y") - moment(XY),
            lambda: lost("z") + moment(XZ),
            lambda: lost("z") - moment(XZ),
            lambda: lost("yz") + moment(YZ),
            lambda: lost("yz") - moment(YZ),
        ]
        for q in which:
            value = post[PLACE[q], p, here, :]
            if q:
                pair = (q - 1) // 2
                if ("pair", pair) not in parts:
                    parts["pair", pair] = rules[pair]()
                value = value - parts["pair", pair]
            post[PLACE[q], p, here, :] = value.astype(jnp.bfloat16).astype(jnp.float32)

    def going(dz, dy):
        return [
            q
            for q, (ex, ey, ez) in enumerate(VELOCITIES)
            if (dz == 0 or ez == dz) and (dy == 0 or ey == dy)
        ]

    def finish_plane(i, carry):
        relax(i, ROW, cy, range(19))
        relax(i, ROW - 1, 1, going(0, 1))
        relax(i, ROW + cy, 1, going(0, -1))
        return carry

    lax.fori_loop(1, cz + 1, finish_plane, 0, unroll=2)
    for p, dz in ((0, 1), (cz + 1, -1)):
        relax(p, ROW, cy, going(dz, 0))
        relax(p, ROW - 1, 1, going(dz, 1))
        relax(p, ROW + cy, 1, going(dz, -1))

    def momentum_plane(i, carry):
        def came(q):
            ex, ey, ez = VELOCITIES[q]
            return post[PLACE[q], i + 1 - ez, pl.ds(ROW - ey, cy), :]

        up = {q: came(q) for q in (1, 7, 9, 11, 13)}
        down = {q: came(q) for q in (2, 8, 10, 12, 14)}
        east = (up[1] + up[7] + up[9] + up[11] + up[13], up[7] - up[9], up[11] - up[13])
        west = (
            down[2] + down[8] + down[10] + down[12] + down[14],
            down[10] - down[8],
            down[14] - down[12],
        )
        d56, d78 = came(15) - came(16), came(17) - came(18)
        jx = roll_x(east[0], 1) - roll_x(west[0], -1)
        jy = (came(3) - came(4)) + (d56 + d78) + (roll_x(east[1], 1) + roll_x(west[1], -1))
        jz = (came(5) - came(6)) + (d56 - d78) + (roll_x(east[2], 1) + roll_x(west[2], -1))
        lines = pl.ds(pl.multiple_of(i * cy, cy), cy)
        lower = pl.ds(pl.multiple_of(nrows + i * cy, cy), cy)
        for n, value in enumerate((jx, jy, jz)):
            high = value.astype(jnp.bfloat16)
            low = (value - high.astype(jnp.float32)).astype(jnp.bfloat16)
            mom[lines, n * cx : (n + 1) * cx] = high
            mom[lower, n * cx : (n + 1) * cx] = low
        return carry

    lax.fori_loop(0, cz, momentum_plane, 0, unroll=2)

    gath[...] = jnp.dot(pick[...], mom[...], preferred_element_type=jnp.float32)

    def parts_of(value):
        first_part = value.astype(jnp.bfloat16)
        return first_part, (value - first_part.astype(jnp.float32)).astype(jnp.bfloat16)

    def dot_t(a, b):
        return lax.dot_general(a, b, (((1,), (1,)), ((), ())), preferred_element_type=jnp.float32)

    ones = jnp.ones((16, cx), jnp.bfloat16)
    forces = []
    for n in range(3):
        acc = None
        for k in range(kk):
            block = pl.ds(k * nmark, nmark)
            term = lanes[block, :] * gath[block, n * cx : (n + 1) * cx]
            acc = term if acc is None else acc + term
        a, b = parts_of(acc)
        forces.append(-(dot_t(ones, a) + dot_t(ones, b))[0:8])
    which = lax.broadcasted_iota(jnp.int32, (8, nmark), 0)
    force = jnp.where(which == 0, forces[0], jnp.where(which == 1, forces[1], forces[2]))
    a, b = parts_of(force)
    both = jnp.concatenate([a.astype(jnp.float32), b.astype(jnp.float32)], axis=0).astype(jnp.bfloat16)
    sums_of = jnp.dot(both, hot[...], preferred_element_type=jnp.float32)
    sums_of = sums_of[0:3] + sums_of[8:11]
    for j in range(ng1):
        h1s[j] = sums_of[:, j * lane_count : (j + 1) * lane_count]

    h1x.start()
    h1r[g1] = h1s[g1]

    def stream_plane(i, carry):
        for q, (ex, ey, ez) in enumerate(VELOCITIES):
            value = post[PLACE[q], i + 1 - ez, pl.ds(ROW - ey, cy), :]
            if ex:
                value = roll_x(value, ex)
            outv[q, i] = value.astype(jnp.bfloat16)
        return carry

    lax.fori_loop(0, cz, stream_plane, 0)
    h1x.all_of().wait_recv()
    total = h1r[0]
    for j in range(1, ng1):
        total = total + h1r[j]
    h2[g2] = total
    h2x.start()

    d1x.all_of().wait_send()
    d2x.all_of().wait_send()
    d3x.all_of().wait_send()
    h1x.all_of().wait_send()

    @pl.when(last)
    def _():
        edges_sent(0)

    @pl.when(first)
    def _():
        edges_sent(1)

    h2x.all_of().wait_recv()
    total = h2[0]
    for j in range(1, ng2):
        total = total + h2[j]
    mine = pltpu.roll(total, (lane_count - place * SEG_DEV) % lane_count, axis=1)
    force_ref[...] = mine[:, 0:SEG_DEV]
    h2x.all_of().wait_send()


def write_kernel(outv, eddy, force, out_hbm, eddy_hbm, force_hbm, sem):
    pieces = sem.shape[0] - 2
    step = -(-outv.shape[0] // pieces)
    copies = []
    for i in range(pieces):
        some = pl.ds(i * step, min(step, outv.shape[0] - i * step))
        copies.append(pltpu.make_async_copy(outv.at[some], out_hbm.at[some], sem.at[i]))
    copies.append(pltpu.make_async_copy(eddy, eddy_hbm, sem.at[pieces]))
    copies.append(pltpu.make_async_copy(force, force_hbm, sem.at[pieces + 1]))
    for copy in copies:
        copy.start()
    for copy in copies:
        copy.wait()


def local(split, populations, cell_index, marker_weight, segment_id):
    nq, cz, cy, cx = populations.shape
    nmark, kk = cell_index.shape
    nz, nx, nc, ny = split
    nxc = nx * nc
    ng1, ng2 = nz * (nx // 2), 2 * nc * ny
    rows = cy // nxc
    f32, bf16 = jnp.float32, jnp.bfloat16
    dma = pltpu.SemaphoreType.DMA
    vmem = pl.BlockSpec(memory_space=pltpu.VMEM)
    hbm = pl.BlockSpec(memory_space=pltpu.HBM)
    lane_count = SEG_DEV * ng2
    velocity, pops = pl.pallas_call(
        functools.partial(velocity_kernel, split),
        out_shape=(
            pltpu.VMEM((3, cz + 4, TOP, cx), f32),
            pltpu.VMEM((nq, cz, cy, cx), bf16),
        ),
        in_specs=[hbm],
        out_specs=(vmem, vmem),
        scratch_shapes=[
            dma((4,)),
            dma((8,)),
            dma((8,)),
        ],
        compiler_params=pltpu.CompilerParams(
            collective_id=0, has_side_effects=True, vmem_limit_bytes=8 * 1024 * 1024
        ),
    )(pltpu.with_memory_space_constraint(populations, pltpu.HBM))
    scratch = [
        pltpu.VMEM((3 * cx, cx), bf16),
        pltpu.VMEM((12, cy, cx), f32),
        pltpu.VMEM((12, cy, cx), f32),
        pltpu.VMEM((cz + 2, 40, cx), f32),
        pltpu.VMEM((12, 40, cx), f32),
        pltpu.VMEM((12, 40, cx), f32),
        pltpu.VMEM((3, 48, cx), f32),
        pltpu.VMEM((3, 48, cx), f32),
        pltpu.VMEM((3, cz + 3, 40, cx), f32),
        pltpu.VMEM((12, cz + 4, cy, cx), f32),
        pltpu.VMEM((2, cy, cx), f32),
        pltpu.VMEM((5, cz + 2, TOP, cx), f32),
        pltpu.VMEM((nq, cz + 2, TOP, cx), f32),
        pltpu.VMEM((TOP, cx), f32),
        pltpu.VMEM((2 * cz * cy, 3 * cx), bf16),
        pltpu.VMEM((kk * nmark, 2 * cz * cy), bf16),
        pltpu.VMEM((kk * nmark, cx), f32),
        pltpu.VMEM((kk * nmark, 3 * cx), f32),
        pltpu.VMEM((nmark, ng1 * lane_count), bf16),
        pltpu.VMEM((nxc, 2 * rows, cx), f32),
        pltpu.VMEM((nxc, 2 * rows, cx), f32),
        pltpu.VMEM((nz, 2 * rows, cx), f32),
        pltpu.VMEM((nxc, rows, cx), f32),
        pltpu.VMEM((rows, cx), f32),
        pltpu.VMEM((rows, cx), f32),
        pltpu.VMEM((ng1, 3, lane_count), f32),
        pltpu.VMEM((ng1, 3, lane_count), f32),
        pltpu.VMEM((ng2, 3, lane_count), f32),
        dma((9,)),
        dma((9,)),
        dma((8,)),
        dma((8,)),
        dma((2,)),
        dma((2,)),
        dma((2,)),
        dma((2,)),
        dma((2,)),
        dma((2,)),
        dma((2,)),
    ]
    results = pl.pallas_call(
        functools.partial(step_kernel, split),
        out_shape=(
            pltpu.VMEM((nq, cz, cy, cx), bf16),
            pltpu.VMEM((cy, cx), f32),
            pltpu.VMEM((3, SEG_DEV), f32),
        ),
        in_specs=[vmem, vmem, vmem, vmem, vmem],
        out_specs=(vmem, vmem, vmem),
        scratch_shapes=scratch,
        compiler_params=pltpu.CompilerParams(
            collective_id=1, has_side_effects=True, vmem_limit_bytes=40 * 1024 * 1024
        ),
    )(velocity, pops, cell_index.T, marker_weight.T, segment_id)
    return pl.pallas_call(
        write_kernel,
        out_shape=(
            jax.ShapeDtypeStruct((nq, cz, cy, cx), bf16),
            jax.ShapeDtypeStruct((cy, cx), f32),
            jax.ShapeDtypeStruct((3, SEG_DEV), f32),
        ),
        in_specs=[vmem, vmem, vmem],
        out_specs=(hbm, hbm, hbm),
        scratch_shapes=[dma((6,))],
        compiler_params=pltpu.CompilerParams(vmem_limit_bytes=1024 * 1024),
    )(*results)


def solution(mesh):
    in_specs = (
        P(None, "span", "cross", None),
        P(("span", "cross"), None),
        P(("span", "cross"), None),
        P(("span", "cross")),
    )
    out_specs = (P(None, "span", "cross", None), P("cross", None), P(None, ("span", "cross")))
    sizes = dict(mesh.shape)
    split = (sizes["span"] // (CHIPS_X * CORES), CHIPS_X, CORES, sizes["cross"])
    return jax.shard_map(
        functools.partial(local, split),
        mesh=mesh,
        in_specs=in_specs,
        out_specs=out_specs,
        check_vma=False,
    )
```

```python
import functools

import jax
import jax.numpy as jnp
from jax import lax
from jax.experimental import pallas as pl
from jax.experimental.pallas import tpu as pltpu
from jax.sharding import PartitionSpec as P

SEG_DEV = 8
MESH = pl.DeviceIdType.MESH
eps_sum = 1e-06
base_visc = 0.005

CHIPS_X = 4
CORES = 2

VELOCITIES = [
    (0, 0, 0),
    (1, 0, 0),
    (-1, 0, 0),
    (0, 1, 0),
    (0, -1, 0),
    (0, 0, 1),
    (0, 0, -1),
    (1, 1, 0),
    (-1, -1, 0),
    (1, -1, 0),
    (-1, 1, 0),
    (1, 0, 1),
    (-1, 0, -1),
    (1, 0, -1),
    (-1, 0, 1),
    (0, 1, 1),
    (0, -1, -1),
    (0, 1, -1),
    (0, -1, 1),
]
ORDER = [18, 5, 11, 14, 15, 3, 7, 10, 17, 6, 12, 13, 16, 4, 8, 9, 0, 1, 2]
PLACE = [ORDER.index(q) for q in range(19)]

ROW = 8
TOP = 48


def add_pairs(f):
    s = [f[2 * i + 1] + f[2 * i + 2] for i in range(9)]
    d = [f[2 * i + 1] - f[2 * i + 2] for i in range(9)]
    return s, d


def tri(low, mid, high):
    return (low + high) + (mid + mid)


def roll_x(a, shift):
    return pltpu.roll(a, shift % a.shape[-1], axis=a.ndim - 1)


def strain_of(d):
    exy, exz, eyz = d[0][1] + d[1][0], d[0][2] + d[2][0], d[1][2] + d[2][1]
    diag = d[0][0] * d[0][0] + d[1][1] * d[1][1] + d[2][2] * d[2][2]
    off = exy * exy + exz * exz + eyz * eyz
    mag = jnp.sqrt(0.5 * diag + 0.25 * off)
    return (d[0][0], d[1][1], d[2][2], exy, exz, eyz), mag


PAIRS = [(0, 0), (1, 1), (2, 2), (0, 1), (0, 2), (1, 2)]


SIDES = [(1, 0), (-1, 0), (0, 1), (0, -1), (1, 1), (1, -1), (-1, 1), (-1, -1)]
XZ, XX, WW, YZ, XY = range(5)


def near(split, dz, dy):
    nz, nx, nc, ny = split
    nspan = nz * nx * nc
    s, y = lax.axis_index("span"), lax.axis_index("cross")
    return ((s + dz + nspan) % nspan, (y + dy + ny) % ny)


def ranges(d, first, size, width):
    if d == 0:
        return pl.ds(first, size), pl.ds(first, size)
    if d > 0:
        return pl.ds(first + size - width, width), pl.ds(first - width, width)
    return pl.ds(first, width), pl.ds(first + size, width)


def kind(i):
    dz, dy = SIDES[i]
    return 2 if dz and dy else (0 if dz else 1)


def velocity_kernel(split, pops_hbm, vel, pops, in_sem, v_send, v_recv):
    cz, cy, cx = pops.shape[1:]
    nchunk = in_sem.shape[0]
    step = cz // nchunk

    def fetch(i):
        some = pl.ds(i * step, step)
        return pltpu.make_async_copy(pops_hbm.at[:, some], pops.at[:, some], in_sem.at[i])

    order = [0, nchunk - 1] + list(range(1, nchunk - 1))
    for i in order:
        fetch(i).start()
    barrier = pltpu.get_barrier_semaphore()
    for dz, dy in SIDES:
        pl.semaphore_signal(
            barrier, inc=1, device_id=near(split, dz, dy), device_id_type=MESH
        )

    def moments_plane(i, carry):
        f = [pops[q, i].astype(jnp.float32) for q in range(19)]
        sm, d = add_pairs(f)
        density = f[0] + ((sm[0] + sm[1] + sm[2]) + (sm[3] + sm[4] + sm[5]) + (sm[6] + sm[7] + sm[8]))
        jx = d[0] + (d[3] + d[4]) + (d[5] + d[6])
        jy = d[1] + (d[3] - d[4]) + (d[7] + d[8])
        jz = d[2] + (d[5] - d[6]) + (d[7] - d[8])
        inv = 1.0 / density
        inner = pl.ds(ROW, cy)
        vel[0, i + 2, inner, :] = jx * inv
        vel[1, i + 2, inner, :] = jy * inv
        vel[2, i + 2, inner, :] = jz * inv
        return carry

    def moments_of(i):
        fetch(i).wait()
        lax.fori_loop(i * step, (i + 1) * step, moments_plane, 0)

    def vel_copy(i):
        dz, dy = SIDES[i]
        zs, zt = ranges(dz, 2, cz, 2)
        ys, yt = ranges(dy, ROW, cy, 2)
        return pltpu.make_async_remote_copy(
            src_ref=vel.at[:, zs, ys, :],
            dst_ref=vel.at[:, zt, yt, :],
            send_sem=v_send.at[kind(i)],
            recv_sem=v_recv.at[kind(i)],
            device_id=near(split, dz, dy),
            device_id_type=MESH,
        )

    for i in order[:2]:
        moments_of(i)
    pl.semaphore_wait(barrier, len(SIDES))
    for i, (dz, dy) in enumerate(SIDES):
        if dz:
            vel_copy(i).start()
    for i in order[2:]:
        moments_of(i)
    for i, (dz, dy) in enumerate(SIDES):
        if not dz:
            vel_copy(i).start()
    inner = pl.ds(ROW, cy)
    wholes = [
        vel.at[:, pl.ds(0, 4), inner, :],
        vel.at[:, pl.ds(2, cz), pl.ds(ROW, 4), :],
        vel.at[:, pl.ds(0, 8), pl.ds(ROW, 2), :],
    ]
    for n, whole in enumerate(wholes):
        pltpu.make_async_remote_copy(
            src_ref=whole,
            dst_ref=whole,
            send_sem=v_send.at[n],
            recv_sem=v_recv.at[n],
            device_id=near(split, 0, 1),
            device_id_type=MESH,
        ).wait()


def step_kernel(
    split,
    vel,
    pops,
    cell_ref,
    weight_ref,
    seg_ref,
    outv,
    eddy_ref,
    force_ref,
    smoother,
    hats_a,
    hats_b,
    mags,
    tmp_a,
    tmp_b,
    vtmp_a,
    vtmp_b,
    vhat,
    filt,
    sums,
    shear,
    post,
    eddyx,
    mom,
    pick,
    lanes,
    gath,
    hot,
    d1s,
    d1r,
    d2,
    d3,
    dlow,
    dhigh,
    h1s,
    h1r,
    h2,
    p_send,
    p_recv,
    d1_sem,
    d2_sem,
    d3_sem,
    e_send,
    e_recv,
    h1_sem,
    h2_sem,
):
    nz, nx, nc, ny = split
    nxc = nx * nc
    cz, cy, cx = pops.shape[1:]
    half = nx // 2
    ng1, ng2 = nz * half, 2 * nc * ny
    s = lax.axis_index("span")
    y = lax.axis_index("cross")
    z, xc = s // nxc, s % nxc
    x, c = xc // nc, xc % nc
    g1 = z * half + x // 2
    g2 = y * (2 * nc) + (x % 2) * nc + c
    place = (x % 2) * (nc * ny) + c * ny + y
    y_up, y_down = (y + 1) % ny, (y + ny - 1) % ny

    def xc_dev(k):
        return (s - xc + (xc + k) % nxc, y)

    def z_dev(k):
        return ((s + nxc * k) % (nz * nxc), y)

    def g1_dev(k):
        return ((s + 2 * nc * k) % (nz * nxc), y)

    def g2_dev(k):
        other = (g2 + k) % ng2
        return (s - s % (2 * nc) + other % (2 * nc), other // (2 * nc))

    def for_others(me, count, act):
        for k in sorted(range(1, count), key=lambda k: abs(2 * k - count)):
            act(k, (me + k) % count)

    def for_all(count, act):
        def body(j, carry):
            act(j)
            return carry

        lax.fori_loop(0, count, body, 0)

    barrier = pltpu.get_barrier_semaphore()

    def greet(dev):
        pl.semaphore_signal(barrier, inc=1, device_id=dev, device_id_type=MESH)

    for_others(g1, ng1, lambda k, j: greet(g1_dev(k)))
    for_others(g2, ng2, lambda k, j: greet(g2_dev(k)))
    for k in range(1, half):
        for t in range(2 * nc):
            greet((z * nxc + ((x // 2 + k) % half) * (2 * nc) + t, y))
    beside_span = [side for side in SIDES if side[0]]
    for dz, dy in beside_span:
        greet(near(split, dz, dy))
    greet((z * nxc + nxc - 1, y_down))
    greet((z * nxc, y_up))
    last, first = xc == nxc - 1, xc == 0
    greeted = len(beside_span) + (half - 1) * 2 * nc + (ng1 - 1) + (ng2 - 1)
    greeted = greeted + jnp.where(jnp.logical_or(last, first), nxc, 0)

    apart = lax.broadcasted_iota(jnp.int32, (cx, cx), 0) - lax.broadcasted_iota(jnp.int32, (cx, cx), 1)
    apart = (apart + cx) % cx
    beside = jnp.logical_or(apart == 1, apart == cx - 1)
    circulant = jnp.where(apart == 0, 2.0 / 64.0, jnp.where(beside, 1.0 / 64.0, 0.0)).astype(jnp.bfloat16)
    for n in range(3):
        smoother[n * cx : (n + 1) * cx, :] = circulant

    def smooth_x(values, count=3):
        rest = jnp.concatenate(values, axis=0)
        parts = []
        for n in range(count):
            parts.append(rest.astype(jnp.bfloat16))
            if n < count - 1:
                rest = rest - parts[-1].astype(jnp.float32)
        parts = jnp.concatenate(parts, axis=1)
        return jnp.dot(parts, smoother[0 : count * cx, :], preferred_element_type=jnp.float32)

    def products(p, tmp, vtmp):
        mid, low, high = pl.ds(ROW - 1, 40), pl.ds(ROW - 2, 40), pl.ds(ROW, 40)
        v = [vel[a, p + 1, mid, :] for a in range(3)]
        for n, (a, b) in enumerate(PAIRS):
            tmp[n + 6] = v[a] * v[b]
        d = []
        for a in range(3):
            below = vel[a, p + 1, low, :]
            vtmp[a, 0:40, :] = tri(vel[a, p, low, :], below, vel[a, p + 2, low, :])
            dx = roll_x(v[a], -1) - roll_x(v[a], 1)
            dy = vel[a, p + 1, high, :] - below
            dz = vel[a, p + 2, mid, :] - vel[a, p, mid, :]
            d.append((dx, dy, dz))
        e, mag = strain_of(d)
        mags[p] = mag
        half_mag = 0.5 * mag
        for n in range(3):
            tmp[n] = mag * e[n]
            tmp[n + 3] = half_mag * e[n + 3]

    def filters(p, tmp, vtmp):
        for n in range(12):
            filt[n, p + 1] = tri(tmp[n, 0:cy, :], tmp[n, 1 : cy + 1, :], tmp[n, 2 : cy + 2, :])
        along_y = [tri(vtmp[a, 0:40, :], vtmp[a, 1:41, :], vtmp[a, 2:42, :]) for a in range(3)]
        smoothed = smooth_x(along_y)
        for a in range(3):
            vhat[a, p + 1] = smoothed[a * 40 : (a + 1) * 40]

    def two_planes(i, carry):
        products(2 * i, tmp_a, vtmp_a)
        filters(2 * i - 1, tmp_b, vtmp_b)
        products(2 * i + 1, tmp_b, vtmp_b)
        filters(2 * i, tmp_a, vtmp_a)
        return carry

    lax.fori_loop(0, (cz + 2) // 2, two_planes, 0)
    filters(cz + 1, tmp_b, vtmp_b)

    def hats_of(i, hats):
        for first_of, parts in ((0, 2), (6, 3)):
            fields = range(first_of, first_of + 6)
            along_z = [tri(filt[n, i + 1], filt[n, i + 2], filt[n, i + 3]) for n in fields]
            smoothed = smooth_x(along_z, parts)
            for n in fields:
                hats[n] = smoothed[(n - first_of) * cy : (n - first_of + 1) * cy]

    def add_plane(i, hats, plane_lm, plane_mm):
        mid, low, high = pl.ds(1, cy), pl.ds(0, cy), pl.ds(2, cy)
        v = [vhat[a, i + 2, mid, :] for a in range(3)]
        d = []
        for a in range(3):
            dx = roll_x(v[a], -1) - roll_x(v[a], 1)
            dy = vhat[a, i + 2, high, :] - vhat[a, i + 2, low, :]
            dz = vhat[a, i + 3, mid, :] - vhat[a, i + 1, mid, :]
            d.append((dx, dy, dz))
        e, mag = strain_of(d)
        four, two = 4.0 * mag, 2.0 * mag
        lm = mm = lm_off = mm_off = None
        for n, (a, b) in enumerate(PAIRS):
            model = hats[n] - (four if n < 3 else two) * e[n]
            leonard = hats[n + 6] - v[a] * v[b]
            if n == 0:
                lm, mm = leonard * model, model * model
            elif n < 3:
                lm, mm = lm + leonard * model, mm + model * model
            elif n == 3:
                lm_off, mm_off = leonard * model, model * model
            else:
                lm_off, mm_off = lm_off + leonard * model, mm_off + model * model
        return plane_lm + (lm + 2.0 * lm_off), plane_mm + (mm + 2.0 * mm_off)

    def second_pass(i, carry):
        hats_of(2 * i + 1, hats_b)
        carry = add_plane(2 * i, hats_a, *carry)
        hats_of(2 * i + 2, hats_a)
        return add_plane(2 * i + 1, hats_b, *carry)

    zero = jnp.zeros((cy, cx), jnp.float32)
    hats_of(0, hats_a)
    plane_lm, plane_mm = lax.fori_loop(0, cz // 2, second_pass, (zero, zero))

    rows = cy // nxc
    sums[0] = plane_lm
    sums[1] = plane_mm
    for j in range(nxc):
        d1s[j, 0:rows, :] = sums[0, j * rows : (j + 1) * rows, :]
        d1s[j, rows : 2 * rows, :] = sums[1, j * rows : (j + 1) * rows, :]

    class Exchange:
        def __init__(self, src, dst, me, count, dev, sems, own):
            self.src, self.dst, self.me, self.count, self.dev = src, dst, me, count, dev
            self.sems, self.own = sems, own

        def copy(self, src, dst, k):
            return pltpu.make_async_remote_copy(
                src_ref=src,
                dst_ref=dst,
                send_sem=self.sems.at[0],
                recv_sem=self.sems.at[1],
                device_id=self.dev(k),
                device_id_type=MESH,
            )

        def start(self):
            def send(k, j):
                self.copy(self.src.at[self.me if self.own else j], self.dst.at[self.me], k).start()

            for_others(self.me, self.count, send)

        def all_of(self):
            some = pl.ds(0, self.count - 1)
            return self.copy(self.src.at[some], self.dst.at[some], 1)

    d1x = Exchange(d1s, d1r, xc, nxc, xc_dev, d1_sem, False)
    d2x = Exchange(d2, d2, z, nz, z_dev, d2_sem, True)
    d3x = Exchange(d3, d3, xc, nxc, xc_dev, d3_sem, True)
    h1x = Exchange(h1s, h1r, g1, ng1, g1_dev, h1_sem, False)
    h2x = Exchange(h2, h2, g2, ng2, g2_dev, h2_sem, True)

    def edge_copy(j, side):
        return pltpu.make_async_remote_copy(
            src_ref=d3.at[xc],
            dst_ref=dlow if side == 0 else dhigh,
            send_sem=e_send.at[side],
            recv_sem=e_recv.at[side],
            device_id=(z * nxc + j, y_up if side == 0 else y_down),
            device_id_type=MESH,
        )

    def edges_sent(side):
        pltpu.make_async_remote_copy(
            src_ref=d3,
            dst_ref=d3,
            send_sem=e_send.at[side],
            recv_sem=e_recv.at[side],
            device_id=(z * nxc, y_up),
            device_id_type=MESH,
        ).wait_send()

    pl.semaphore_wait(barrier, greeted)
    d1x.start()

    inner = pl.ds(ROW, cy)

    def collide_plane(i, carry):
        f = [pops[q, i].astype(jnp.float32) for q in range(19)]
        sm, d = add_pairs(f)
        sx, sy, sz, sa, sb, sc, sd, se, sg = sm
        dx, dy, dz, da, db, dc, dd, de, dg = d
        ux, uy, uz = [vel[a, i + 2, inner, :] for a in range(3)]
        xy, xz, yz = sa + sb, sc + sd, se + sg
        axis, diag = sx + sy + sz, xy + xz + yz
        abp, abm, cdp, cdm, egp, egm = da + db, da - db, dc + dd, dc - dd, de + dg, de - dg
        jx, jy, jz = dx + (abp + cdp), dy + (abm + egp), dz + (cdm + egm)
        jxx, jyy, jzz = jx * ux, jy * uy, jz * uz
        ju = jxx + jyy + jzz
        ne = (1.19 * 19.0 / 2394.0) * (diag - f[0] - ju)
        neps = (1.4 / 252.0) * (9.0 * f[0] - 7.0 * axis - 2.0 * diag + 5.5 * ju)
        ax_part = -11.0 * ne - 4.0 * neps
        dg_part = 8.0 * ne + neps
        eq_xx = 3.0 * jxx - ju
        eq_ww = jyy - jzz
        axis_xx, diag_xx = 3.0 * sx - axis, diag - 3.0 * yz
        axis_ww, diag_ww = sy - sz, xy - xz
        pi_xx = (1.4 / 72.0) * (diag_xx - 2.0 * axis_xx + 0.5 * eq_xx)
        pi_ww = (1.4 / 24.0) * (diag_ww - 2.0 * axis_ww + 0.5 * eq_ww)
        shear[XX, i + 1, inner, :] = (1.0 / 36.0) * (axis_xx + diag_xx - eq_xx)
        shear[WW, i + 1, inner, :] = (1.0 / 12.0) * (axis_ww + diag_ww - eq_ww)
        shear[XY, i + 1, inner, :] = 0.25 * (sa - sb - jx * uy)
        shear[XZ, i + 1, inner, :] = 0.25 * (sc - sd - jx * uz)
        shear[YZ, i + 1, inner, :] = 0.25 * (se - sg - jy * uz)
        two_xx, two_ww = 2.0 * pi_xx, 2.0 * pi_ww
        base_yz = ax_part + two_xx
        hx = ax_part - 2.0 * two_xx
        hy, hz = base_yz - two_ww, base_yz + two_ww
        base_d = dg_part + pi_xx
        hxy, hxz, hyz = base_d + pi_ww, base_d - pi_ww, dg_part - two_xx
        tx = (1.2 / 8.0) * ((1.0 / 3.0) * jx - dx)
        ty = (1.2 / 8.0) * ((1.0 / 3.0) * jy - dy)
        tz = (1.2 / 8.0) * ((1.0 / 3.0) * jz - dz)
        mx = (1.98 / 8.0) * (abp - cdp)
        my = (1.98 / 8.0) * (egp - abm)
        mz = (1.98 / 8.0) * (cdm - egm)
        xp, xm, yp, ym, zp, zm = tx + mx, tx - mx, ty + my, ty - my, tz + mz, tz - mz
        halves = [
            (hx, -4.0 * tx),
            (hy, -4.0 * ty),
            (hz, -4.0 * tz),
            (hxy, xp + ym),
            (hxy, xp - ym),
            (hxz, xm + zp),
            (hxz, xm - zp),
            (hyz, yp + zm),
            (hyz, yp - zm),
        ]
        post[PLACE[0], i + 1, inner, :] = f[0] + (30.0 * ne - 12.0 * neps)
        for n, (even, odd) in enumerate(halves):
            post[PLACE[2 * n + 1], i + 1, inner, :] = f[2 * n + 1] - (even + odd)
            post[PLACE[2 * n + 2], i + 1, inner, :] = f[2 * n + 2] - (even - odd)
        return carry

    lax.fori_loop(0, cz, collide_plane, 0)

    crossing = [
        ((1, 0), 0, 5),
        ((-1, 0), 8, 5),
        ((0, 1), 4, 5),
        ((0, -1), 12, 4),
        ((0, -1), 0, 1),
        ((1, 1), 4, 1),
        ((1, -1), 0, 1),
        ((-1, 1), 8, 1),
        ((-1, -1), 12, 1),
    ]

    def halo_copy(ref, side, first_of, count, send, recv):
        dz, dy = side
        zs, zt = ranges(dz, 1, cz, 1)
        ys, yt = ranges(dy, ROW, cy, 1)
        group = pl.ds(first_of, count)
        return pltpu.make_async_remote_copy(
            src_ref=ref.at[group, zs, ys, :],
            dst_ref=ref.at[group, zt, yt, :],
            send_sem=send,
            recv_sem=recv,
            device_id=near(split, dz, dy),
            device_id_type=MESH,
        )

    halo = []
    for side, first_of, count in crossing:
        n = kind(SIDES.index(side))
        halo.append(halo_copy(post, side, first_of, count, p_send.at[n], p_recv.at[n]))
    for i, side in enumerate(SIDES):
        first_of = 0 if side[1] == 0 else (1 if side[0] == 0 else 1)
        count = 3 if side[0] and side[1] else 4
        n = 3 + kind(i)
        halo.append(halo_copy(shear, side, first_of, count, p_send.at[n], p_recv.at[n]))

    for copy in halo:
        copy.start()

    d1r[xc] = d1s[xc]
    d1x.all_of().wait_recv()
    total = d1r[0]
    for j in range(1, nxc):
        total = total + d1r[j]
    d2[z] = total
    d2x.start()

    kk, nmark = cell_ref.shape
    nrows = cz * cy
    nhalf = nrows // 2
    row_iota = lax.broadcasted_iota(jnp.int32, (nmark, nhalf), 1)
    lane_iota = lax.broadcasted_iota(jnp.int32, (nmark, cx), 1)
    cells = jnp.transpose(cell_ref[...], (1, 0))
    weights = jnp.transpose(weight_ref[...], (1, 0))
    for k in range(kk):
        cell = cells[:, k : k + 1]
        line = cell // cx
        block = pl.ds(k * nmark, nmark)
        for h in range(2):
            picked = jnp.where(row_iota == line - h * nhalf, 1.0, 0.0).astype(jnp.bfloat16)
            pick[block, h * nrows : h * nrows + nhalf] = picked
            pick[block, h * nrows + nhalf : (h + 1) * nrows] = picked
        lanes[block, :] = jnp.where(lane_iota == cell - line * cx, weights[:, k : k + 1], 0.0)
    ids = jnp.broadcast_to(seg_ref[...].reshape(1, nmark), (8, nmark))
    ids = jnp.transpose(ids, (1, 0))[:, 0:1]
    lane_count = SEG_DEV * ng2
    seg_iota = lax.broadcasted_iota(jnp.int32, (nmark, lane_count), 1)
    for j in range(ng1):
        hot[:, j * lane_count : (j + 1) * lane_count] = jnp.where(
            seg_iota == ids - j * lane_count, 1.0, 0.0
        ).astype(jnp.bfloat16)

    d2x.all_of().wait_recv()
    total = d2[0]
    for j in range(1, nz):
        total = total + d2[j]
    d1s[xc] = total
    eddy_rows = jnp.maximum(d1s[xc, 0:rows, :] / (d1s[xc, rows : 2 * rows, :] + eps_sum), 0.0)
    d3[xc] = eddy_rows
    d3x.start()

    @pl.when(last)
    def _():
        for_all(nxc, lambda j: edge_copy(j, 0).start())

    @pl.when(first)
    def _():
        for_all(nxc, lambda j: edge_copy(j, 1).start())

    wholes = [
        post.at[pl.ds(0, 10), pl.ds(1, 1), inner, :],
        post.at[pl.ds(0, 10), pl.ds(1, cz), pl.ds(ROW, 1), :],
        post.at[pl.ds(0, 4), pl.ds(1, 1), pl.ds(ROW, 1), :],
        shear.at[pl.ds(0, 4), pl.ds(1, 2), inner, :],
        shear.at[pl.ds(0, 4), pl.ds(1, cz), pl.ds(ROW, 2), :],
        shear.at[pl.ds(0, 3), pl.ds(1, 4), pl.ds(ROW, 1), :],
    ]
    for n, whole in enumerate(wholes):
        pltpu.make_async_remote_copy(
            src_ref=whole,
            dst_ref=whole,
            send_sem=p_send.at[n],
            recv_sem=p_recv.at[n],
            device_id=near(split, 0, 1),
            device_id_type=MESH,
        ).wait()
    d3x.all_of().wait_recv()
    for side in range(2):
        edge_copy(0, side).wait_recv()
    for j in range(nxc):
        eddy_ref[j * rows : (j + 1) * rows, :] = d3[j]
        eddyx[ROW + j * rows : ROW + (j + 1) * rows, :] = d3[j]
    eddyx[ROW - 1 : ROW, :] = dlow[rows - 1 : rows, :]
    eddyx[ROW + cy : ROW + cy + 1, :] = dhigh[0:1, :]

    def relax(p, start, count, which):
        here = pl.ds(start, count)
        mag = mags[p, pl.ds(start - ROW + 1, count), :]
        rate = 1.0 / (0.5 + 3.0 * (base_visc + eddyx[here, :] * mag))
        parts = {}

        def moment(n):
            if n not in parts:
                parts[n] = rate * shear[n, p, here, :]
            return parts[n]

        def lost(n):
            if n in parts:
                return parts[n]
            if n == "y":
                value = moment(XX) + moment(WW)
            elif n == "z":
                value = moment(XX) - moment(WW)
            else:
                value = -2.0 * moment(XX)
            parts[n] = value
            return value

        rules = [
            lambda: 2.0 * moment(XX),
            lambda: moment(WW) - moment(XX),
            lambda: -lost("y"),
            lambda: lost("y") + moment(XY),
            lambda: lost("y") - moment(XY),
            lambda: lost("z") + moment(XZ),
            lambda: lost("z") - moment(XZ),
            lambda: lost("yz") + moment(YZ),
            lambda: lost("yz") - moment(YZ),
        ]
        for q in which:
            value = post[PLACE[q], p, here, :]
            if q:
                pair = (q - 1) // 2
                if ("pair", pair) not in parts:
                    parts["pair", pair] = rules[pair]()
                value = value - parts["pair", pair]
            post[PLACE[q], p, here, :] = value.astype(jnp.bfloat16).astype(jnp.float32)

    def going(dz, dy):
        return [
            q
            for q, (ex, ey, ez) in enumerate(VELOCITIES)
            if (dz == 0 or ez == dz) and (dy == 0 or ey == dy)
        ]

    def finish_plane(i, carry):
        relax(i, ROW, cy, range(19))
        relax(i, ROW - 1, 1, going(0, 1))
        relax(i, ROW + cy, 1, going(0, -1))
        return carry

    lax.fori_loop(1, cz + 1, finish_plane, 0, unroll=4)
    for p, dz in ((0, 1), (cz + 1, -1)):
        relax(p, ROW, cy, going(dz, 0))
        relax(p, ROW - 1, 1, going(dz, 1))
        relax(p, ROW + cy, 1, going(dz, -1))

    def momentum_plane(h, i):
        def came(q):
            ex, ey, ez = VELOCITIES[q]
            return post[PLACE[q], i + 1 - ez, pl.ds(ROW - ey, cy), :]

        up = {q: came(q) for q in (1, 7, 9, 11, 13)}
        down = {q: came(q) for q in (2, 8, 10, 12, 14)}
        east = (up[1] + up[7] + up[9] + up[11] + up[13], up[7] - up[9], up[11] - up[13])
        west = (
            down[2] + down[8] + down[10] + down[12] + down[14],
            down[10] - down[8],
            down[14] - down[12],
        )
        d56, d78 = came(15) - came(16), came(17) - came(18)
        jx = roll_x(east[0], 1) - roll_x(west[0], -1)
        jy = (came(3) - came(4)) + (d56 + d78) + (roll_x(east[1], 1) + roll_x(west[1], -1))
        jz = (came(5) - came(6)) + (d56 - d78) + (roll_x(east[2], 1) + roll_x(west[2], -1))
        line = (i - h * (cz // 2)) * cy + h * nrows
        if not isinstance(line, int):
            line = pl.multiple_of(line, cy)
        lines, lower = pl.ds(line, cy), pl.ds(line + nhalf, cy)
        for n, value in enumerate((jx, jy, jz)):
            high = value.astype(jnp.bfloat16)
            low = (value - high.astype(jnp.float32)).astype(jnp.bfloat16)
            mom[lines, n * cx : (n + 1) * cx] = high
            mom[lower, n * cx : (n + 1) * cx] = low

    def first_half(i, carry):
        momentum_plane(0, i)
        return carry

    lax.fori_loop(0, cz // 2, first_half, 0, unroll=min(4, cz // 2))

    def gathered(h):
        lines = pl.ds(h * nrows, nrows)
        return jnp.dot(pick[:, lines], mom[lines, :], preferred_element_type=jnp.float32)

    gath[0] = gathered(0)
    for i in range(cz // 2, cz):
        momentum_plane(1, i)
    gath[1] = gathered(1)

    def parts_of(value):
        first_part = value.astype(jnp.bfloat16)
        return first_part, (value - first_part.astype(jnp.float32)).astype(jnp.bfloat16)

    def dot_t(a, b):
        return lax.dot_general(a, b, (((1,), (1,)), ((), ())), preferred_element_type=jnp.float32)

    ones = jnp.ones((16, cx), jnp.bfloat16)
    forces = []
    for n in range(3):
        acc = None
        for k in range(kk):
            block = pl.ds(k * nmark, nmark)
            here = pl.ds(n * cx, cx)
            term = lanes[block, :] * (gath[0, block, here] + gath[1, block, here])
            acc = term if acc is None else acc + term
        a, b = parts_of(acc)
        forces.append(-(dot_t(ones, a) + dot_t(ones, b))[0:8])
    which = lax.broadcasted_iota(jnp.int32, (8, nmark), 0)
    force = jnp.where(which == 0, forces[0], jnp.where(which == 1, forces[1], forces[2]))
    a, b = parts_of(force)
    both = jnp.concatenate([a.astype(jnp.float32), b.astype(jnp.float32)], axis=0).astype(jnp.bfloat16)
    sums_of = jnp.dot(both, hot[...], preferred_element_type=jnp.float32)
    sums_of = sums_of[0:3] + sums_of[8:11]
    for j in range(ng1):
        h1s[j] = sums_of[:, j * lane_count : (j + 1) * lane_count]

    h1x.start()
    h1r[g1] = h1s[g1]

    def stream_plane(i, carry):
        for q, (ex, ey, ez) in enumerate(VELOCITIES):
            value = post[PLACE[q], i + 1 - ez, pl.ds(ROW - ey, cy), :]
            if ex:
                value = roll_x(value, ex)
            outv[q, i] = value.astype(jnp.bfloat16)
        return carry

    lax.fori_loop(0, cz, stream_plane, 0)
    h1x.all_of().wait_recv()
    total = h1r[0]
    for j in range(1, ng1):
        total = total + h1r[j]
    h2[g2] = total
    h2x.start()

    d1x.all_of().wait_send()
    d2x.all_of().wait_send()
    d3x.all_of().wait_send()
    h1x.all_of().wait_send()

    @pl.when(last)
    def _():
        edges_sent(0)

    @pl.when(first)
    def _():
        edges_sent(1)

    h2x.all_of().wait_recv()
    total = h2[0]
    for j in range(1, ng2):
        total = total + h2[j]
    mine = pltpu.roll(total, (lane_count - place * SEG_DEV) % lane_count, axis=1)
    force_ref[...] = mine[:, 0:SEG_DEV]
    h2x.all_of().wait_send()


def write_kernel(outv, eddy, force, out_hbm, eddy_hbm, force_hbm, sem):
    pieces = sem.shape[0] - 2
    step = -(-outv.shape[0] // pieces)
    copies = []
    for i in range(pieces):
        some = pl.ds(i * step, min(step, outv.shape[0] - i * step))
        copies.append(pltpu.make_async_copy(outv.at[some], out_hbm.at[some], sem.at[i]))
    copies.append(pltpu.make_async_copy(eddy, eddy_hbm, sem.at[pieces]))
    copies.append(pltpu.make_async_copy(force, force_hbm, sem.at[pieces + 1]))
    for copy in copies:
        copy.start()
    for copy in copies:
        copy.wait()


def local(split, populations, cell_index, marker_weight, segment_id):
    nq, cz, cy, cx = populations.shape
    nmark, kk = cell_index.shape
    nz, nx, nc, ny = split
    nxc = nx * nc
    ng1, ng2 = nz * (nx // 2), 2 * nc * ny
    rows = cy // nxc
    f32, bf16 = jnp.float32, jnp.bfloat16
    dma = pltpu.SemaphoreType.DMA
    vmem = pl.BlockSpec(memory_space=pltpu.VMEM)
    hbm = pl.BlockSpec(memory_space=pltpu.HBM)
    lane_count = SEG_DEV * ng2
    velocity, pops = pl.pallas_call(
        functools.partial(velocity_kernel, split),
        out_shape=(
            pltpu.VMEM((3, cz + 4, TOP, cx), f32),
            pltpu.VMEM((nq, cz, cy, cx), bf16),
        ),
        in_specs=[hbm],
        out_specs=(vmem, vmem),
        scratch_shapes=[
            dma((4,)),
            dma((3,)),
            dma((3,)),
        ],
        compiler_params=pltpu.CompilerParams(
            collective_id=0, has_side_effects=True, vmem_limit_bytes=8 * 1024 * 1024
        ),
    )(pltpu.with_memory_space_constraint(populations, pltpu.HBM))
    scratch = [
        pltpu.VMEM((3 * cx, cx), bf16),
        pltpu.VMEM((12, cy, cx), f32),
        pltpu.VMEM((12, cy, cx), f32),
        pltpu.VMEM((cz + 2, 40, cx), f32),
        pltpu.VMEM((12, 40, cx), f32),
        pltpu.VMEM((12, 40, cx), f32),
        pltpu.VMEM((3, 48, cx), f32),
        pltpu.VMEM((3, 48, cx), f32),
        pltpu.VMEM((3, cz + 3, 40, cx), f32),
        pltpu.VMEM((12, cz + 4, cy, cx), f32),
        pltpu.VMEM((2, cy, cx), f32),
        pltpu.VMEM((5, cz + 2, TOP, cx), f32),
        pltpu.VMEM((nq, cz + 2, TOP, cx), f32),
        pltpu.VMEM((TOP, cx), f32),
        pltpu.VMEM((2 * cz * cy, 3 * cx), bf16),
        pltpu.VMEM((kk * nmark, 2 * cz * cy), bf16),
        pltpu.VMEM((kk * nmark, cx), f32),
        pltpu.VMEM((2, kk * nmark, 3 * cx), f32),
        pltpu.VMEM((nmark, ng1 * lane_count), bf16),
        pltpu.VMEM((nxc, 2 * rows, cx), f32),
        pltpu.VMEM((nxc, 2 * rows, cx), f32),
        pltpu.VMEM((nz, 2 * rows, cx), f32),
        pltpu.VMEM((nxc, rows, cx), f32),
        pltpu.VMEM((rows, cx), f32),
        pltpu.VMEM((rows, cx), f32),
        pltpu.VMEM((ng1, 3, lane_count), f32),
        pltpu.VMEM((ng1, 3, lane_count), f32),
        pltpu.VMEM((ng2, 3, lane_count), f32),
        dma((6,)),
        dma((6,)),
        dma((2,)),
        dma((2,)),
        dma((2,)),
        dma((2,)),
        dma((2,)),
        dma((2,)),
        dma((2,)),
    ]
    results = pl.pallas_call(
        functools.partial(step_kernel, split),
        out_shape=(
            pltpu.VMEM((nq, cz, cy, cx), bf16),
            pltpu.VMEM((cy, cx), f32),
            pltpu.VMEM((3, SEG_DEV), f32),
        ),
        in_specs=[vmem, vmem, vmem, vmem, vmem],
        out_specs=(vmem, vmem, vmem),
        scratch_shapes=scratch,
        compiler_params=pltpu.CompilerParams(
            collective_id=1, has_side_effects=True, vmem_limit_bytes=40 * 1024 * 1024
        ),
    )(velocity, pops, cell_index.T, marker_weight.T, segment_id)
    return pl.pallas_call(
        write_kernel,
        out_shape=(
            jax.ShapeDtypeStruct((nq, cz, cy, cx), bf16),
            jax.ShapeDtypeStruct((cy, cx), f32),
            jax.ShapeDtypeStruct((3, SEG_DEV), f32),
        ),
        in_specs=[vmem, vmem, vmem],
        out_specs=(hbm, hbm, hbm),
        scratch_shapes=[dma((6,))],
        compiler_params=pltpu.CompilerParams(vmem_limit_bytes=1024 * 1024),
    )(*results)


def solution(mesh):
    in_specs = (
        P(None, "span", "cross", None),
        P(("span", "cross"), None),
        P(("span", "cross"), None),
        P(("span", "cross")),
    )
    out_specs = (P(None, "span", "cross", None), P("cross", None), P(None, ("span", "cross")))
    sizes = dict(mesh.shape)
    split = (sizes["span"] // (CHIPS_X * CORES), CHIPS_X, CORES, sizes["cross"])
    return jax.shard_map(
        functools.partial(local, split),
        mesh=mesh,
        in_specs=in_specs,
        out_specs=out_specs,
        check_vma=False,
    )
```
